32 devices in a mesh: seq: 8 (over z, y), head: 4 (over x, core).
Axes of the slice: x: 2, y: 2, z: 4, core: 2. Of those that a mesh axis runs over, the one named last changes fastest.
Arguments:
- tokens: bfloat16 [4, 4096, 1024], P(None, 'seq'), may hold values from -6 to 6
- cotangent: bfloat16 [4, 4096, 1024], P(None, 'seq'), may hold values from -6 to 6
- mixer_norm: float32 [1024], replicated, may hold values from 0.5 to 1.5
- query_weight: bfloat16 [1024, 512], P(None, 'head'), may hold values from -0.1875 to 0.1875
- key_weight: bfloat16 [1024, 512], P(None, 'head'), may hold values from -0.1875 to 0.1875
- value_weight: bfloat16 [1024, 1024], P(None, 'head'), may hold values from -0.1875 to 0.1875
- gate_weight: bfloat16 [1024, 1024], P(None, 'head'), may hold values from -0.1875 to 0.1875
- decay_down: bfloat16 [1024, 16], replicated, may hold values from -0.1875 to 0.1875
- decay_up: float32 [16, 512], P(None, 'head'), may hold values from -1.5 to 1.5
- decay_bias: float32 [512], P('head'), may hold values from -1 to 9
- query_conv: float32 [4, 512], P(None, 'head'), may hold values from -3 to 3
- key_conv: float32 [4, 512], P(None, 'head'), may hold values from -3 to 3
- value_conv: float32 [4, 1024], P(None, 'head'), may hold values from -3 to 3
- group_gain: float32 [1024], P('head'), may hold values from 0.5 to 1.5
- output_weight: bfloat16 [1024, 1024], P('head'), may hold values from -0.1875 to 0.1875
- feed_norm: float32 [1024], replicated, may hold values from 0.5 to 1.5
- feed_gate: bfloat16 [1024, 2816], P(None, 'head'), may hold values from -0.1875 to 0.1875
- feed_up: bfloat16 [1024, 2816], P(None, 'head'), may hold values from -0.1875 to 0.1875
- feed_down: bfloat16 [2816, 1024], P('head'), may hold values from -0.109375 to 0.109375
Outputs:
- layer_out: bfloat16 [4, 4096, 1024], P(None, 'seq')
- token_grad: float32 [4, 4096, 1024], P(None, 'seq')
- mixer_norm_grad: float32 [1024], replicated
- query_weight_grad: float32 [1024, 512], P('seq', 'head')
- key_weight_grad: float32 [1024, 512], P('seq', 'head')
- value_weight_grad: float32 [1024, 1024], P('seq', 'head')
- gate_weight_grad: float32 [1024, 1024], P('seq', 'head')
- decay_down_grad: float32 [1024, 16], P('seq')
- decay_up_grad: float32 [16, 512], P(None, 'head')
- decay_bias_grad: float32 [512], P('head')
- query_conv_grad: float32 [4, 512], P(None, 'head')
- key_conv_grad: float32 [4, 512], P(None, 'head')
- value_conv_grad: float32 [4, 1024], P(None, 'head')
- group_gain_grad: float32 [1024], P('head')
- output_weight_grad: float32 [1024, 1024], P('head', 'seq')
- feed_norm_grad: float32 [1024], replicated
- feed_gate_grad: float32 [1024, 2816], P('seq', 'head')
- feed_up_grad: float32 [1024, 2816], P('seq', 'head')
- feed_down_grad: float32 [2816, 1024], P('head', 'seq')
The draws below stay inside these ranges and needn't reach their ends.
All inputs are finite; a program needn't handle non-finite values.
Results may differ from the reference program's by a relative error of at most 0.012.
The reference program's roundings to bfloat16 on the way (of `normed`, `gated` and `inner`) count: a program that leaves them out, or rounds other values in their place, can miss the bound.
Values may be sent and summed in bfloat16 or wider, within the bound.
No kernel may reach another device: no remote copies, remote signals or barrier semaphores. Data moves between devices by JAX's collectives and lax.ppermute only.
A program may use at most 256 MiB of HBM per device.

```python
import jax
import jax.numpy as jnp
from jax import lax

D = 1024
HEADS = 4
KH = 128
VH = 256
FF = 2816
RANK = 16
STRETCH = 64
CONV = 4
SEQS = 4
LEN = 4096
KEYS = 512
VALS = 1024


def draw_decay_bias(key, part):
    key = jax.random.fold_in(key, 11)
    pick_key, fast_key, slow_key = jax.random.split(key, 3)
    selector = jax.random.uniform(pick_key, (KEYS,), jnp.float32) < 0.5
    fast_bias = jax.random.uniform(fast_key, (KEYS,), jnp.float32, minval=-1.0, maxval=2.0)
    slow_bias = jax.random.uniform(slow_key, (KEYS,), jnp.float32, minval=6.0, maxval=9.0)
    return jnp.where(selector, fast_bias, slow_bias).astype(jnp.float32)


def shard_levels(stream_key, dims, cuts, smallest, top_value):
    gain, own = 1.0, jax.random.fold_in(stream_key, 6)
    for dim, parts in cuts:
        draws = jnp.exp(jax.random.uniform(jax.random.fold_in(own, dim), (parts,), jnp.float32, smallest / len(cuts), top_value / len(cuts)))
        gain = gain * jnp.repeat(draws, dims[dim] // parts).reshape([-1 if axis == dim else 1 for axis in range(len(dims))])
    return gain


def bell_draw(key, shape, spread, reach, shards=(), kind=jnp.bfloat16):
    values = spread * jax.random.normal(key, shape, jnp.float32)
    if shards:
        values = values * shard_levels(key, shape, shards, -0.22, 0.18)
    return jnp.clip(values, -reach, reach).astype(kind)


def setup_inputs(seed: int = 0) -> dict:
    splits = jax.random.split(jax.random.key(seed), 20)
    return {
        "tokens": bell_draw(splits[0], (SEQS, LEN, D), 1.0, 6.0, ((1, 8),)),
        "cotangent": bell_draw(splits[1], (SEQS, LEN, D), 1.0, 6.0, ((1, 8),)),
        "mixer_norm": jnp.clip(1.0 + 0.1 * jax.random.normal(splits[2], (D,), jnp.float32), 0.5, 1.5),
        "query_weight": bell_draw(splits[3], (D, KEYS), D ** -0.5, 0.1875, ((1, 4),)),
        "key_weight": bell_draw(splits[4], (D, KEYS), D ** -0.5, 0.1875, ((1, 4),)),
        "value_weight": bell_draw(splits[5], (D, VALS), D ** -0.5, 0.1875, ((1, 4),)),
        "gate_weight": bell_draw(splits[6], (D, VALS), D ** -0.5, 0.1875, ((1, 4),)),
        "decay_down": bell_draw(splits[7], (D, RANK), D ** -0.5, 0.1875),
        "decay_up": bell_draw(splits[8], (RANK, KEYS), RANK ** -0.5, 1.5, ((1, 4),), jnp.float32),
        "decay_bias": draw_decay_bias(jax.random.fold_in(splits[19], 71), 0),
        "query_conv": bell_draw(splits[10], (CONV, KEYS), CONV ** -0.5, 3.0, ((1, 4),), jnp.float32),
        "key_conv": bell_draw(splits[11], (CONV, KEYS), CONV ** -0.5, 3.0, ((1, 4),), jnp.float32),
        "value_conv": bell_draw(splits[12], (CONV, VALS), CONV ** -0.5, 3.0, ((1, 4),), jnp.float32),
        "group_gain": jnp.clip(1.0 + 0.1 * jax.random.normal(splits[13], (VALS,), jnp.float32), 0.5, 1.5),
        "output_weight": bell_draw(splits[14], (VALS, D), VALS ** -0.5, 0.1875, ((0, 4),)),
        "feed_norm": jnp.clip(1.0 + 0.1 * jax.random.normal(splits[15], (D,), jnp.float32), 0.5, 1.5),
        "feed_gate": bell_draw(splits[16], (D, FF), D ** -0.5, 0.1875, ((1, 4),)),
        "feed_up": bell_draw(splits[17], (D, FF), D ** -0.5, 0.1875, ((1, 4),)),
        "feed_down": bell_draw(splits[18], (FF, D), FF ** -0.5, 0.109375, ((0, 4),)),
    }


highest = lax.Precision.HIGHEST
epsilon = 1e-06

@jax.custom_vjp
def low(v):
    return lax.optimization_barrier(v.astype(jnp.bfloat16)).astype(jnp.float32)

@jax.custom_vjp
def low_back(v):
    return v

def low_keep(v):
    return (low(v), None)

def low_pass(kept, grad):
    return (grad,)

def back_keep(v):
    return (v, None)

def back_low(kept, grad):
    return (low(grad),)
low.defvjp(low_keep, low_pass)
low_back.defvjp(back_keep, back_low)

def rounded(values):
    return low(low_back(values))

def matmul(left, right):
    return jnp.einsum('...i,ij->...j', left, right, precision=highest)

def rms_scale(values):
    return lax.rsqrt(lax.optimization_barrier(jnp.mean(values * values, axis=-1, keepdims=True)) + epsilon)

def short_conv(inputs, kernel):
    padded = jnp.pad(inputs, ((0, 0), (CONV - 1, 0), (0, 0)))
    span_len = inputs.shape[1]
    summed = kernel[0] * padded[:, 0:span_len, :]
    for offset in range(1, CONV):
        summed = summed + kernel[offset] * padded[:, offset:offset + span_len, :]
    return summed

def block_step(current, pieces):
    queries, key_vecs, val_vecs, logdec = pieces
    span_len = queries.shape[1]
    cumulative = jnp.cumsum(logdec, axis=1)
    middle = cumulative[:, span_len // 2 - 1:span_len // 2]
    ahead_vecs = queries * jnp.exp(cumulative - middle)
    behind_vecs = key_vecs * jnp.exp(middle - cumulative)
    causal = jnp.tril(jnp.ones((span_len, span_len), jnp.float32))
    scores = jnp.einsum('schk,sthk->shct', ahead_vecs, behind_vecs, precision=highest) * causal
    intra_part = jnp.einsum('shct,sthv->schv', scores, val_vecs, precision=highest)
    inter_part = jnp.einsum('schk,shkv->schv', queries * jnp.exp(cumulative), current, precision=highest)
    last_cum = cumulative[:, -1]
    carried = key_vecs * jnp.exp(last_cum[:, None] - cumulative)
    updated = jnp.exp(last_cum)[..., None] * current + jnp.einsum('schk,schv->shkv', carried, val_vecs, precision=highest)
    return (updated, intra_part + inter_part)

def attention(queries, key_vecs, val_vecs, logdec):
    blocks = LEN // STRETCH

    def split(values):
        return jnp.moveaxis(values.reshape((SEQS, blocks, STRETCH) + values.shape[2:]), 1, 0)
    start_state = jnp.zeros((SEQS, HEADS, KH, VH), jnp.float32)
    _, produced = lax.scan(jax.checkpoint(block_step), start_state, (split(queries), split(key_vecs), split(val_vecs), split(logdec)))
    return jnp.moveaxis(produced, 0, 1).reshape(SEQS, LEN, HEADS, VH)

def forward(tokens_f, mixer_norm, query_weight, key_weight, value_weight, gate_weight, decay_down, decay_up, decay_bias, query_conv, key_conv, value_conv, group_gain, output_weight, feed_norm, feed_gate, feed_up, feed_down):
    normed = low(tokens_f * rms_scale(tokens_f) * mixer_norm)
    query_pre = rounded(matmul(normed, query_weight))
    key_pre = rounded(matmul(normed, key_weight))
    value_pre = rounded(matmul(normed, value_weight))
    gate_pre = low_back(matmul(normed, gate_weight))
    latent = low_back(matmul(normed, decay_down))
    logits = matmul(latent, decay_up) + decay_bias
    logdec = (jax.nn.log_sigmoid(logits) / 16.0).reshape(SEQS, LEN, HEADS, KH)
    queries = (low(jax.nn.silu(short_conv(query_pre, query_conv))) * KH ** (-0.5)).reshape(SEQS, LEN, HEADS, KH)
    key_vecs = low(jax.nn.silu(short_conv(key_pre, key_conv))).reshape(SEQS, LEN, HEADS, KH)
    val_vecs = low(jax.nn.silu(short_conv(value_pre, value_conv))).reshape(SEQS, LEN, HEADS, VH)
    attended = attention(queries, key_vecs, val_vecs, logdec)
    normed_heads = attended * rms_scale(attended) * group_gain.reshape(HEADS, VH)
    gated = low(normed_heads.reshape(SEQS, LEN, VALS) * jax.nn.silu(gate_pre))
    mixer_out = low_back(matmul(gated, output_weight))
    hidden_one = tokens_f + mixer_out
    normed_two = low(hidden_one * rms_scale(hidden_one) * feed_norm)
    gate_two = low_back(matmul(normed_two, feed_gate))
    up_two = low_back(matmul(normed_two, feed_up))
    inner = low(jax.nn.silu(gate_two) * up_two)
    feed_out = low_back(matmul(inner, feed_down))
    return hidden_one + feed_out

def reference(tokens, cotangent, mixer_norm, query_weight, key_weight, value_weight, gate_weight, decay_down, decay_up, decay_bias, query_conv, key_conv, value_conv, group_gain, output_weight, feed_norm, feed_gate, feed_up, feed_down):
    inputs = (tokens, mixer_norm, query_weight, key_weight, value_weight, gate_weight, decay_down, decay_up, decay_bias, query_conv, key_conv, value_conv, group_gain, output_weight, feed_norm, feed_gate, feed_up, feed_down)
    floats = jax.tree.map(lambda array_in: array_in.astype(jnp.float32), inputs)
    layer, pull = jax.vjp(forward, *floats)
    grads = pull(cotangent.astype(jnp.float32))
    return (layer.astype(jnp.bfloat16), grads[0], grads[1], grads[2], grads[3], grads[4], grads[5], grads[6], grads[7], grads[8], grads[9], grads[10], grads[11], grads[12], grads[13], grads[14], grads[15], grads[16], grads[17])
```

```python
import functools

import jax
import jax.numpy as jnp
from jax import lax
from jax.experimental import pallas as pl
from jax.experimental.pallas import tpu as pltpu
from jax.sharding import PartitionSpec as P

KH = 128
VH = 256
STRETCH = 64
CONV = 4
SCALE = KH**-0.5
PAD = 8

epsilon = 1e-06
highest = lax.Precision.HIGHEST
f32 = jnp.float32
bf16 = jnp.bfloat16
VMEM = 50 * 1024 * 1024
SENT_IN = f32
SENT_OUT = bf16


def dot(a, b, dims=((1,), (0,)), precision=None):
    return lax.dot_general(a, b, (dims, ((), ())), precision=precision, preferred_element_type=f32)


NT = ((1,), (1,))
TN = ((0,), (0,))


def split_dot(left, values, dims=((1,), (0,))):
    high = values.astype(bf16)
    low = (values - high.astype(f32)).astype(bf16)
    return dot(left, high, dims) + dot(left, low, dims)


def two_pieces(values):
    high = values.astype(bf16)
    return high, (values - high.astype(f32)).astype(bf16)


def lower(span, strict=False):
    row = lax.broadcasted_iota(jnp.int32, (span, span), 0)
    col = lax.broadcasted_iota(jnp.int32, (span, span), 1)
    return (row > col) if strict else (row >= col)


def as_bf(mask):
    return jnp.where(mask, 1.0, 0.0).astype(bf16)


def call(body, grid, ins, outs, scratch=(), flops=1e9, moved=4e6, prefetch=0):
    arrays = [entry[0] if isinstance(entry, tuple) else entry for entry in ins]
    in_specs = [
        pl.BlockSpec(memory_space=pltpu.SMEM) if entry[1] is None else pl.BlockSpec(entry[1], entry[2])
        for entry in ins[prefetch:]
    ]
    return pl.pallas_call(
        body,
        out_shape=[jax.ShapeDtypeStruct(entry[0], entry[1]) for entry in outs],
        grid_spec=pltpu.PrefetchScalarGridSpec(
            num_scalar_prefetch=prefetch,
            grid=grid,
            in_specs=in_specs,
            out_specs=[pl.BlockSpec(entry[2], entry[3]) for entry in outs],
            scratch_shapes=list(scratch),
        ),
        compiler_params=pltpu.CompilerParams(vmem_limit_bytes=VMEM),
        cost_estimate=pl.CostEstimate(
            flops=int(flops), bytes_accessed=int(moved), transcendentals=0
        ),
    )(*arrays)


def whole(array):
    zeros = (0,) * array.ndim
    return (array, array.shape, lambda *_: zeros)


def by_slot(array):
    rest = (0,) * (array.ndim - 1)
    return (array, (None,) + array.shape[1:], lambda i, *_: (i,) + rest)


def at_slot(array, slot):
    rest = (0,) * (array.ndim - 1)
    return (array, (None,) + array.shape[1:], lambda *_: (slot,) + rest)


def out_by_slot(shape, dtype):
    rest = (0,) * (len(shape) - 1)
    return (shape, dtype, (None,) + shape[1:], lambda i, *_: (i,) + rest)


def out_whole(shape, dtype):
    zeros = (0,) * len(shape)
    return (shape, dtype, shape, lambda *_: zeros)


def project_body(
    order, tokens, gain, w_query, w_key, w_value, w_gate, w_down, normed, pre, gate_pre, latent
):
    values = tokens[...].astype(f32)
    scaled = values * lax.rsqrt(jnp.mean(values * values, axis=-1, keepdims=True) + epsilon)
    low = (scaled * gain[...]).astype(bf16)
    normed[...] = low
    keys, vals = w_query.shape[1], w_value.shape[1]
    pre[:, :keys] = dot(low, w_query[...]).astype(bf16)
    pre[:, keys : 2 * keys] = dot(low, w_key[...]).astype(bf16)
    pre[:, 2 * keys :] = dot(low, w_value[...]).astype(bf16)
    gate_pre[...] = dot(low, w_gate[...])
    latent[...] = dot(low, w_down[...])


def conv_sum(scratch, taps, rows):
    summed = taps[0:1, :] * scratch[pl.ds(PAD - CONV + 1, rows), :]
    for offset in range(1, CONV):
        summed = summed + taps[offset : offset + 1, :] * scratch[
            pl.ds(PAD - CONV + 1 + offset, rows), :
        ]
    return summed


def decay_logits(latent, up, bias):
    return dot(latent[...], up[...], precision=highest) + bias[...]


def conv_body(
    pre, halo, taps, latent, up, bias, queries, key_vecs, val_vecs, inner_sum, starts, states, message, ext
):
    rows = pre.shape[0]
    ext[0:PAD, :] = halo[...].astype(f32)
    ext[PAD : PAD + rows, :] = pre[...].astype(f32)
    summed = conv_sum(ext, taps[...], rows)
    active = (summed * jax.nn.sigmoid(summed)).astype(bf16)
    queries[...] = active[:, :KH]
    key_vecs[...] = active[:, KH : 2 * KH]
    val_vecs[...] = active[:, 2 * KH :]
    logits = decay_logits(latent, up, bias)
    logdec = (jnp.minimum(logits, 0.0) - jnp.log1p(jnp.exp(-jnp.abs(logits)))) * (1.0 / 16.0)
    tril = jnp.where(lower(STRETCH), 1.0, 0.0)
    state = jnp.zeros((VH, KH), f32)
    before = jnp.zeros((1, KH), f32)
    for block in range(rows // STRETCH):
        at = slice(block * STRETCH, (block + 1) * STRETCH)
        total = dot(tril, logdec[at], precision=highest)
        inner_sum[at, :] = total
        last = total[STRETCH - 1 : STRETCH]
        starts[block : block + 1, :] = before
        states[block] = state
        carried = (active[at, KH : 2 * KH].astype(f32) * jnp.exp(last - total)).astype(bf16)
        state = state * jnp.exp(last) + dot(active[at, 2 * KH :], carried, TN)
        before = before + last
    message[0:VH, :] = state.astype(message.dtype)
    message[VH:, :] = jnp.broadcast_to(jnp.exp(before), (16, KH)).astype(message.dtype)


def halves(total):
    middle = total[STRETCH // 2 - 1 : STRETCH // 2]
    return jnp.exp(total - middle), jnp.exp(middle - total)


def local_body(queries, key_vecs, val_vecs, inner_sum, states, attended):
    mask = lower(STRETCH)
    for block in range(queries.shape[0] // STRETCH):
        at = slice(block * STRETCH, (block + 1) * STRETCH)
        total = inner_sum[at, :]
        query = queries[at, :].astype(f32) * SCALE
        up, down = halves(total)
        ahead = (query * up).astype(bf16)
        behind = (key_vecs[at, :].astype(f32) * down).astype(bf16)
        scores = jnp.where(mask, dot(ahead, behind, NT), 0.0).astype(bf16)
        entering, rest = two_pieces(query * jnp.exp(total))
        high, low = two_pieces(states[block])
        attended[at, :] = (
            dot(scores, val_vecs[at, :])
            + dot(entering, high, NT)
            + dot(entering, low, NT)
            + dot(rest, high, NT)
        )


def device_sum(inner_sum, starts):
    rows = inner_sum.shape[0]
    return jnp.concatenate(
        [
            inner_sum[block * STRETCH : (block + 1) * STRETCH, :] + starts[block : block + 1, :]
            for block in range(rows // STRETCH)
        ],
        axis=0,
    )


def mix_body(
    local, queries, inner_sum, starts, incoming, gate_pre, gain, w_out, attended, gated, mixed
):
    total = device_sum(inner_sum, starts)
    entering, rest = two_pieces(queries[...].astype(f32) * SCALE * jnp.exp(total))
    high, low = two_pieces(incoming[...])
    values = local[...] + dot(entering, high, NT) + dot(entering, low, NT) + dot(rest, high, NT)
    attended[...] = values
    scaled = values * lax.rsqrt(jnp.mean(values * values, axis=-1, keepdims=True) + epsilon)
    gate = gate_pre[...]
    low = (scaled * gain[...] * (gate * jax.nn.sigmoid(gate))).astype(bf16)
    gated[...] = low
    mixed[...] = dot(low, w_out[...]).astype(mixed.dtype)


def feed_body(
    normed, cotangent, w_gate, w_up, w_down, inner, grad_gate, grad_up, grad_normed, feed_out
):
    low = normed[...]
    gate = dot(low, w_gate[...])
    up = dot(low, w_up[...])
    grad = dot(cotangent[...], w_down[...], NT)
    soft = jax.nn.sigmoid(gate)
    silu = gate * soft
    product = (silu * up).astype(bf16)
    inner[...] = product
    gate_low = (grad * up * (soft * (1.0 + gate * (1.0 - soft)))).astype(bf16)
    up_low = (grad * silu).astype(bf16)
    grad_gate[...] = gate_low
    grad_up[...] = up_low
    feed_out[...] = dot(product, w_down[...]).astype(feed_out.dtype)
    summed = dot(gate_low, w_gate[...], NT) + dot(up_low, w_up[...], NT)
    grad_normed[...] = summed.astype(grad_normed.dtype)


def gate_back_body(
    grad_hidden, w_out, attended, gate_pre, gain, queries, inner_sum, starts,
    grad_attended, grad_gate, gain_part, message,
):
    grad = dot(grad_hidden[...], w_out[...], NT)
    values = attended[...]
    inverse = lax.rsqrt(jnp.mean(values * values, axis=-1, keepdims=True) + epsilon)
    scaled = values * inverse
    gate = gate_pre[...]
    soft = jax.nn.sigmoid(gate)
    grad_gate[...] = (
        grad * scaled * gain[...] * (soft * (1.0 + gate * (1.0 - soft)))
    ).astype(bf16)
    grad = grad * (gate * soft)
    gain_part[...] = jnp.broadcast_to(jnp.sum(grad * scaled, axis=0, keepdims=True), gain_part.shape)
    grad = grad * gain[...]
    grad = inverse * (grad - scaled * jnp.mean(grad * scaled, axis=-1, keepdims=True))
    grad_attended[...] = grad
    high, low = two_pieces(grad)
    total = device_sum(inner_sum, starts)
    entering = (queries[...].astype(f32) * SCALE * jnp.exp(total)).astype(bf16)
    message[...] = (dot(high, entering, TN) + dot(low, entering, TN)).astype(message.dtype)


def local_back_body(
    queries, key_vecs, val_vecs, inner_sum, starts, states, incoming, grad_attended,
    grad_queries, grad_keys, grad_vals, grad_logdec,
):
    mask = lower(STRETCH)
    row = lax.broadcasted_iota(jnp.int32, (STRETCH, 2 * STRETCH), 0)
    col = lax.broadcasted_iota(jnp.int32, (STRETCH, 2 * STRETCH), 1)
    later = jnp.where(col >= row, 1.0, 0.0)
    earlier = jnp.where(col - STRETCH < row, 1.0, 0.0)
    sums = jnp.where(col < STRETCH, later, earlier).astype(bf16)
    running = jnp.zeros((VH, KH), f32)
    entered = incoming[...]
    for block in reversed(range(queries.shape[0] // STRETCH)):
        at = slice(block * STRETCH, (block + 1) * STRETCH)
        total = inner_sum[at, :]
        last = total[STRETCH - 1 : STRETCH]
        query = queries[at, :].astype(f32) * SCALE
        key = key_vecs[at, :].astype(f32)
        val = val_vecs[at, :]
        grad, grad_rest = two_pieces(grad_attended[at, :])
        up, down = halves(total)
        whole_up = jnp.exp(total)
        rest = jnp.exp(last - total)
        ahead = (query * up).astype(bf16)
        behind = (key * down).astype(bf16)
        entering = (query * whole_up).astype(bf16)
        carried = (key * rest).astype(bf16)
        current = states[block] + entered * jnp.exp(starts[block : block + 1, :])
        scores = jnp.where(mask, dot(ahead, behind, NT), 0.0).astype(bf16)
        grad_scores = jnp.where(mask, dot(grad, val, NT) + dot(grad_rest, val, NT), 0.0).astype(bf16)
        running_low, running_rest = two_pieces(running)
        current_low, current_rest = two_pieces(current)
        grad_ahead = dot(grad_scores, behind)
        grad_behind = dot(grad_scores, ahead, TN)
        grad_entering = (
            dot(grad, current_low) + dot(grad, current_rest) + dot(grad_rest, current_low)
        )
        grad_carried = dot(val, running_low) + dot(val, running_rest)
        grad_vals[at, :] = dot(scores, grad, TN) + dot(carried, running_low, NT)
        grad_queries[at, :] = (grad_ahead * up + grad_entering * whole_up) * SCALE
        grad_keys[at, :] = grad_behind * down + grad_carried * rest
        inside = (
            ahead.astype(f32) * grad_ahead
            - behind.astype(f32) * grad_behind
            + entering.astype(f32) * grad_entering
        )
        stacked = jnp.concatenate([inside, carried.astype(f32) * grad_carried], axis=0)
        through = jnp.sum(current * running, axis=0, keepdims=True) * jnp.exp(last)
        grad_logdec[at, :] = split_dot(sums, stacked) + through
        running = running * jnp.exp(last) + dot(grad, entering, TN) + dot(grad_rest, entering, TN)


def conv_back_body(
    grad_queries, grad_keys, grad_vals, grad_logdec, key_vecs, val_vecs, inner_sum, starts,
    incoming, outgoing, pre, halo, taps, latent, up, bias,
    grad_pre, tail, head, taps_part, bias_part, up_part, grad_latent, ext, back,
):
    rows = pre.shape[0]
    keys = grad_queries.shape[1]
    ext[0:PAD, :] = halo[...].astype(f32)
    ext[PAD : PAD + rows, :] = pre[...].astype(f32)
    summed = conv_sum(ext, taps[...], rows)
    soft = jax.nn.sigmoid(summed)
    slope = soft * (1.0 + summed * (1.0 - soft))
    total = device_sum(inner_sum, starts)
    final = total[rows - 1 : rows]
    rest = jnp.exp(final - total)
    leaving, leaving_rest = two_pieces(outgoing[...])
    carried = (key_vecs[...].astype(f32) * rest).astype(bf16)
    grad_carried = dot(val_vecs[...], leaving) + dot(val_vecs[...], leaving_rest)
    back[0:PAD, :] = jnp.zeros((PAD, back.shape[1]), f32)
    back[PAD + rows :, :] = jnp.zeros((PAD, back.shape[1]), f32)
    back[PAD : PAD + rows, 0:keys] = grad_queries[...] * slope[:, 0:keys]
    back[PAD : PAD + rows, keys : 2 * keys] = (grad_keys[...] + grad_carried * rest) * slope[
        :, keys : 2 * keys
    ]
    back[PAD : PAD + rows, 2 * keys :] = (grad_vals[...] + dot(carried, leaving, NT)) * slope[
        :, 2 * keys :
    ]
    pairs = carried.astype(f32) * grad_carried
    strict = as_bf(lower(STRETCH, True))
    through = jnp.sum(incoming[...] * outgoing[...], axis=0, keepdims=True) * jnp.exp(final)
    logits = decay_logits(latent, up, bias)
    fade = jax.nn.sigmoid(-logits) * (1.0 / 16.0)
    pieces = []
    for block in range(rows // STRETCH):
        at = slice(block * STRETCH, (block + 1) * STRETCH)
        pieces.append(grad_logdec[at, :] + split_dot(strict, pairs[at]) + through)
        through = through + jnp.sum(pairs[at], axis=0, keepdims=True)
    grad_logits = jnp.concatenate(pieces, axis=0) * fade
    bias_part[...] = jnp.broadcast_to(
        jnp.sum(grad_logits, axis=0, keepdims=True), bias_part.shape
    )
    up_part[...] = dot(latent[...], grad_logits, TN, highest)
    grad_latent[...] = dot(up[...], grad_logits, NT, highest)
    kernel = taps[...]
    grad = kernel[0:1, :] * back[pl.ds(CONV - 1, PAD + rows), :]
    for offset in range(1, CONV):
        grad = grad + kernel[offset : offset + 1, :] * back[
            pl.ds(CONV - 1 - offset, PAD + rows), :
        ]
    head[...] = grad[0:PAD]
    tail[...] = grad[rows:]
    grad_pre[...] = grad[PAD:].astype(bf16)
    inner = back[PAD : PAD + rows, :]
    for offset in range(CONV):
        taps_part[offset : offset + 1, :] = jnp.sum(
            inner * ext[pl.ds(PAD - CONV + 1 + offset, rows), :], axis=0, keepdims=True
        )


def project_back_body(
    grad_pre, tail, arrived, grad_gate, w_query, w_key, w_value, w_gate, fixed, grad_normed
):
    rows = grad_pre.shape[0]
    keys = w_query.shape[1]
    fixed[0 : rows - 16, :] = grad_pre[0 : rows - 16, :]
    ending = jnp.concatenate(
        [grad_pre[rows - 16 : rows, :].astype(f32)[0 : 16 - PAD], tail[...] + arrived[...]], axis=0
    )
    fixed[rows - 16 : rows, :] = ending.astype(bf16)
    low = fixed[...]
    summed = dot(low[:, 0:keys], w_query[...], NT) + dot(low[:, keys : 2 * keys], w_key[...], NT)
    summed = summed + dot(low[:, 2 * keys :], w_value[...], NT)
    summed = summed + dot(grad_gate[...], w_gate[...], NT)
    grad_normed[...] = summed.astype(grad_normed.dtype)


def weight_grads(jobs, width, blocks=4):
    arrays, plan = [], []
    depth = None
    for left, right, first in jobs:
        entry = []
        for side, group in ((0, left), (1, right)):
            places = []
            for array in group if isinstance(group, list) else [group]:
                known = [k for k, (other, s) in enumerate(arrays) if other is array and s == side]
                if not known:
                    arrays.append((array, side))
                    known = [len(arrays) - 1]
                places.append(known[0])
            entry.append(places)
        plan.append((entry[0], entry[1], first))
    first_left = jobs[0][0][0] if isinstance(jobs[0][0], list) else jobs[0][0]
    depth = first_left.shape[-1]
    block = depth // blocks

    def body(*refs):
        out = refs[-1]
        covered = 0
        for lefts, rights, first in plan:
            total = None
            for left, right in zip(lefts, rights):
                a, b = refs[left], refs[right]
                pairs = (
                    [(a, b)]
                    if len(a.shape) == 2
                    else [(a.at[k], b.at[k]) for k in range(a.shape[0])]
                )
                for one, two in pairs:
                    term = dot(one[...], two[...], TN)
                    total = term if total is None else total + term
            if first > covered:
                out[:, covered:first] = jnp.zeros((block, first - covered), bf16)
            out[:, first : first + total.shape[1]] = total.astype(bf16)
            covered = first + total.shape[1]
        if covered < width:
            out[:, covered:] = jnp.zeros((block, width - covered), bf16)

    ins = []
    flops, moved = 0, depth * width * 2
    for array, side in arrays:
        moved += array.size * 2
        if side == 1:
            ins.append(whole(array))
        elif array.ndim == 2:
            ins.append((array, (array.shape[0], block), lambda i: (0, i)))
        else:
            ins.append((array, array.shape[:2] + (block,), lambda i: (0, 0, i)))
    rows = first_left.shape[-2] * 4
    flops = 2 * rows * depth * width
    return call(
        body,
        (blocks,),
        ins,
        [((depth, width), bf16, (block, width), lambda i: (i, 0))],
        flops=flops,
        moved=moved,
    )[0]


def bits_of(axis):
    count = lax.axis_size(axis)
    return [1 << k for k in range(count.bit_length() - 1)]


def swap(value, axis, bit):
    count = lax.axis_size(axis)
    return lax.ppermute(value, axis, [(source, source ^ bit) for source in range(count)])


def passed_along(value, axis, steps):
    count = lax.axis_size(axis)
    first, last = (max(0, -steps), min(count, count - steps))
    return lax.ppermute(value, axis, [(source, source + steps) for source in range(first, last)])


def exchange_states(message, reverse, decays=None):
    place = lax.axis_index("seq")
    state = message[:, :VH].astype(f32)
    result = jnp.zeros_like(state)
    passed = jnp.ones((message.shape[0], 1, KH), f32)
    decay = None if reverse else message[:, VH : VH + 1].astype(f32)
    kept = []
    sent = message
    bits = bits_of("seq")
    for level, bit in enumerate(bits):
        other = swap(sent, "seq", bit)
        upper = (place // bit) % 2 == 1
        theirs = other[:, :VH].astype(f32)
        if reverse:
            passed, low_decay = decays[level]
            adds = jnp.logical_not(upper)
        else:
            their_decay = other[:, VH : VH + 1].astype(f32)
            low_decay = jnp.where(upper, their_decay, decay)
            high_decay = jnp.where(upper, decay, their_decay)
            adds = upper
        result = result + jnp.where(adds, passed * theirs, 0.0)
        if not reverse:
            passed_next = jnp.where(upper, passed * their_decay, passed)
        if level + 1 < len(bits):
            if reverse:
                first = jnp.where(upper, theirs, state)
                second = jnp.where(upper, state, theirs)
                state = first + low_decay * second
                sent = state.astype(message.dtype)
            else:
                first = jnp.where(upper, theirs, state)
                second = jnp.where(upper, state, theirs)
                state = high_decay * first + second
                both = low_decay * high_decay
                sent = jnp.concatenate(
                    [state, jnp.broadcast_to(both, (state.shape[0], 16, KH))], axis=1
                ).astype(message.dtype)
        if not reverse:
            kept.append((upper, decay, their_decay))
            passed = passed_next
            decay = low_decay * high_decay
    return result, kept


def reverse_decays(kept):
    levels = []
    after = None
    for upper, own, theirs in kept:
        if after is None:
            after = jnp.ones_like(own)
        levels.append((after, jnp.where(upper, theirs, own)))
        after = jnp.where(upper, after, after * theirs)
    return levels


def total_sum(value, axes):
    for axis in axes:
        for bit in bits_of(axis):
            value = value + swap(value, axis, bit)
    return value


def scatter_sum(value, axis):
    place = lax.axis_index(axis)
    parts = lax.axis_size(axis)
    columns = value.shape[1]
    block = value.shape[0] // parts
    current = value
    for bit in bits_of(axis):
        mine = (place // bit) % 2
        pairs = current.reshape(parts // (2 * bit), 2, block, columns)
        kept = lax.dynamic_index_in_dim(pairs, mine, 1, False)
        sent = lax.dynamic_index_in_dim(pairs, 1 - mine, 1, False)
        got = swap(sent.astype(bf16), axis, bit)
        current = kept.astype(f32) + got.astype(f32)
        if 2 * bit < parts:
            current = current.astype(bf16)
    return current.reshape(block, columns)


def gather_slots(own):
    one = swap(own, "head", 1)
    two = swap(own, "head", 2)
    three = swap(two, "head", 1)
    return [own, one, two, three]


def norm_back(values, gain_vec, grad):
    inverse = lax.rsqrt(jnp.mean(values * values, axis=-1, keepdims=True) + epsilon)
    scaled = values * inverse
    gain_part = jnp.sum(grad * scaled, axis=0)
    inner = grad * gain_vec
    return inverse * (inner - scaled * jnp.mean(inner * scaled, axis=-1, keepdims=True)), gain_part


def shards(
    tokens,
    cotangent,
    mixer_norm,
    query_weight,
    key_weight,
    value_weight,
    gate_weight,
    decay_down,
    decay_up,
    decay_bias,
    query_conv,
    key_conv,
    value_conv,
    group_gain,
    output_weight,
    feed_norm,
    feed_gate,
    feed_up,
    feed_down,
):
    slots, rows, width = tokens.shape
    keys = query_weight.shape[1]
    vals = value_weight.shape[1]
    hidden = feed_gate.shape[1]
    rank = decay_down.shape[1]
    all_cols = 2 * keys + vals
    blocks = rows // STRETCH
    assert slots == lax.axis_size("head") == 4 and keys == KH and vals == VH
    me = lax.axis_index("head")
    order = jnp.bitwise_xor(jnp.arange(slots, dtype=jnp.int32), me.astype(jnp.int32))

    def sequence(array, slot):
        return lax.dynamic_index_in_dim(array, order[slot], 0, False)

    def restored(pieces):
        result = jnp.zeros((slots,) + pieces[0].shape, pieces[0].dtype)
        for slot, piece in enumerate(pieces):
            result = lax.dynamic_update_index_in_dim(result, piece, order[slot], 0)
        return result

    taps = jnp.concatenate([query_conv, key_conv, value_conv], axis=-1)
    gain_row = group_gain.reshape(1, vals)
    bias_row = decay_bias.reshape(1, keys)

    normed, pre, gate_pre, latent = call(
        project_body,
        (slots,),
        [
            order,
            (tokens, (None, rows, width), lambda i, order_ref: (order_ref[i], 0, 0)),
            whole(mixer_norm.reshape(1, width)),
            whole(query_weight),
            whole(key_weight),
            whole(value_weight),
            whole(gate_weight),
            whole(decay_down),
        ],
        [
            out_by_slot((slots, rows, width), bf16),
            out_by_slot((slots, rows, all_cols), bf16),
            out_by_slot((slots, rows, vals), f32),
            out_by_slot((slots, rows, rank), f32),
        ],
        flops=2 * slots * rows * width * (all_cols + vals + rank),
        moved=2 * slots * rows * (2 * width + all_cols + 2 * vals),
        prefetch=1,
    )
    halo = passed_along(pre[:, rows - PAD :, :], "seq", 1)
    queries, key_vecs, val_vecs, inner_sum, starts, states, message = call(
        conv_body,
        (slots,),
        [
            by_slot(pre),
            by_slot(halo),
            whole(taps),
            by_slot(latent),
            whole(decay_up),
            whole(bias_row),
        ],
        [
            out_by_slot((slots, rows, keys), bf16),
            out_by_slot((slots, rows, keys), bf16),
            out_by_slot((slots, rows, vals), bf16),
            out_by_slot((slots, rows, keys), f32),
            out_by_slot((slots, blocks, keys), f32),
            out_by_slot((slots, blocks, VH, KH), f32),
            out_by_slot((slots, VH + 16, KH), SENT_IN),
        ],
        [pltpu.VMEM((PAD + rows, all_cols), f32)],
        flops=4e9,
        moved=10e6,
    )
    (local,) = call(
        local_body,
        (slots,),
        [by_slot(a) for a in (queries, key_vecs, val_vecs, inner_sum, states)],
        [out_by_slot((slots, rows, vals), f32)],
        flops=6e9,
        moved=8e6,
    )
    incoming, kept = exchange_states(message, False)

    attended, gated, mixed = [None] * 4, [None] * 4, [None] * 4
    for slot in (3, 2, 1, 0):
        attended[slot], gated[slot], mixed[slot] = call(
            mix_body,
            (1,),
            [at_slot(a, slot) for a in (local, queries, inner_sum, starts, incoming, gate_pre)]
            + [whole(gain_row), whole(output_weight)],
            [
                out_whole((rows, vals), f32),
                out_whole((rows, vals), bf16),
                out_whole((rows, width), bf16 if slot % 2 else f32),
            ],
            flops=2 * rows * vals * (width + keys),
            moved=4e6,
        )
    def reduced(parts):
        far = swap(parts[3], "head", 1)
        far = swap((parts[2] + far.astype(f32)).astype(bf16), "head", 2)
        near = swap(parts[1], "head", 1)
        return parts[0] + near.astype(f32) + far.astype(f32)

    hidden_share = sequence(tokens, 0).astype(f32) + reduced(mixed)
    second = (
        hidden_share
        * lax.rsqrt(jnp.mean(hidden_share * hidden_share, axis=-1, keepdims=True) + epsilon)
        * feed_norm
    ).astype(bf16)
    second_all = gather_slots(second)

    cots = [sequence(cotangent, slot) for slot in range(slots)]
    inner, grad_gates, grad_ups, grad_seconds, feed_outs = ([None] * 4 for _ in range(5))
    tile = min(256, rows)
    for slot in (0, 1, 2, 3):
        wide = bf16 if slot % 2 else f32
        rowed = lambda i: (i, 0)
        inner[slot], grad_gates[slot], grad_ups[slot], grad_seconds[slot], feed_outs[slot] = call(
            feed_body,
            (rows // tile,),
            [
                (second_all[slot], (tile, width), rowed),
                (cots[slot], (tile, width), rowed),
                whole(feed_gate),
                whole(feed_up),
                whole(feed_down),
            ],
            [
                ((rows, hidden), bf16, (tile, hidden), rowed),
                ((rows, hidden), bf16, (tile, hidden), rowed),
                ((rows, hidden), bf16, (tile, hidden), rowed),
                ((rows, width), wide, (tile, width), rowed),
                ((rows, width), wide, (tile, width), rowed),
            ],
            flops=12 * rows * width * hidden,
            moved=12e6,
        )
    grad_second_share = reduced(grad_seconds)
    grad_norm_share, feed_norm_part = norm_back(hidden_share, feed_norm, grad_second_share)
    grad_hidden_share = cots[0].astype(f32) + grad_norm_share
    grad_low = gather_slots(grad_hidden_share.astype(bf16))

    padded = -(-hidden // 128) * 128
    feed_pack = weight_grads(
        [
            (second_all, grad_gates, 0),
            (second_all, grad_ups, padded),
            (cots, inner, 2 * padded),
        ],
        3 * padded,
    )
    feed_scattered = lax.psum_scatter(feed_pack, "seq", scatter_dimension=0, tiled=True)

    grad_attended, grad_gate, gain_parts, messages = ([None] * 4 for _ in range(4))
    for slot in (0, 1, 2, 3):
        grad_attended[slot], grad_gate[slot], gain_parts[slot], messages[slot] = call(
            gate_back_body,
            (1,),
            [whole(grad_low[slot]), whole(output_weight), whole(attended[slot])]
            + [at_slot(gate_pre, slot), whole(gain_row)]
            + [at_slot(a, slot) for a in (queries, inner_sum, starts)],
            [
                out_whole((rows, vals), f32),
                out_whole((rows, vals), bf16),
                out_whole((8, vals), f32),
                out_whole((VH, KH), SENT_OUT),
            ],
            flops=2 * rows * vals * (width + keys),
            moved=4e6,
        )
    outgoing, _ = exchange_states(jnp.stack(messages), True, reverse_decays(kept))
    grad_local = call(
        local_back_body,
        (slots,),
        [
            by_slot(a)
            for a in (
                queries, key_vecs, val_vecs, inner_sum, starts, states, incoming,
                jnp.stack(grad_attended),
            )
        ],
        [
            out_by_slot((slots, rows, keys), f32),
            out_by_slot((slots, rows, keys), f32),
            out_by_slot((slots, rows, vals), f32),
            out_by_slot((slots, rows, keys), f32),
        ],
        flops=15e9,
        moved=14e6,
    )
    grad_pre, tail, head, taps_part, bias_part, up_part, grad_latent = call(
        conv_back_body,
        (slots,),
        [by_slot(a) for a in grad_local]
        + [by_slot(a) for a in (key_vecs, val_vecs, inner_sum, starts, incoming, outgoing)]
        + [by_slot(pre), by_slot(halo), whole(taps), by_slot(latent), whole(decay_up)]
        + [whole(bias_row)],
        [
            out_by_slot((slots, rows, all_cols), bf16),
            out_by_slot((slots, PAD, all_cols), f32),
            out_by_slot((slots, PAD, all_cols), f32),
            out_by_slot((slots, CONV, all_cols), f32),
            out_by_slot((slots, 8, keys), f32),
            out_by_slot((slots, rank, keys), f32),
            out_by_slot((slots, rank, rows), f32),
        ],
        [
            pltpu.VMEM((PAD + rows, all_cols), f32),
            pltpu.VMEM((2 * PAD + rows, all_cols), f32),
        ],
        flops=8e9,
        moved=14e6,
    )
    arrived = passed_along(head, "seq", -1)

    fixed, grad_normed = [None] * 4, [None] * 4
    for slot in (3, 2, 1, 0):
        fixed[slot], grad_normed[slot] = call(
            project_back_body,
            (1,),
            [at_slot(a, slot) for a in (grad_pre, tail, arrived)]
            + [whole(grad_gate[slot])]
            + [whole(w) for w in (query_weight, key_weight, value_weight, gate_weight)],
            [
                out_whole((rows, all_cols), bf16),
                out_whole((rows, width), bf16 if slot % 2 else f32),
            ],
            flops=2 * rows * width * (all_cols + vals),
            moved=4e6,
        )
    latent_slots = total_latent(grad_latent)
    latent_low = latent_slots.astype(bf16)
    grad_normed_share = reduced(grad_normed) + lax.dot_general(
        latent_low, decay_down, (((0,), (1,)), ((), ())), preferred_element_type=f32
    )
    own_tokens = sequence(tokens, 0).astype(f32)
    grad_token_norm, mixer_norm_part = norm_back(own_tokens, mixer_norm, grad_normed_share)
    token_share = (grad_hidden_share + grad_token_norm).astype(bf16)
    token_grad = restored([piece.astype(f32) for piece in gather_slots(token_share)])

    layer_share = (hidden_share + reduced(feed_outs)).astype(bf16)
    layer_out = restored(gather_slots(layer_share))

    down_part = lax.dot_general(
        normed[0], latent_low, (((0,), (1,)), ((), ())), preferred_element_type=f32
    )
    side_pack = weight_grads([(grad_low, gated, 0), ([normed], [jnp.stack(grad_gate)], vals)], 2 * vals)
    side_scattered = scatter_sum(side_pack, "seq")
    pre_pack = weight_grads([([normed], [jnp.stack(fixed)], 0)], all_cols)
    pre_scattered = scatter_sum(pre_pack, "seq")
    down_scattered = total_sum(scatter_sum(down_part.astype(f32), "seq"), ("head",))

    def tall(value):
        return value.reshape(-1, 128)

    gain_part = sum(part[0] for part in gain_parts)
    taps_sum = jnp.sum(taps_part, axis=0)
    small = jnp.concatenate(
        [
            tall(gain_part),
            tall(bias_part[:, 0].sum(axis=0)),
            tall(up_part.sum(axis=0)),
            tall(taps_sum),
        ],
        axis=0,
    )
    small = total_sum(small, ("seq",)).reshape(-1)
    cuts = [vals, vals + keys, vals + keys + rank * keys]
    group_gain_grad = small[: cuts[0]]
    decay_bias_grad = small[cuts[0] : cuts[1]]
    decay_up_grad = small[cuts[1] : cuts[2]].reshape(rank, keys)
    taps_grad = small[cuts[2] :].reshape(CONV, all_cols)
    norms = jnp.concatenate([tall(mixer_norm_part), tall(feed_norm_part)], axis=0)
    norms = total_sum(norms, ("head", "seq")).reshape(2, width)

    return (
        layer_out,
        token_grad,
        norms[0],
        pre_scattered[:, :keys],
        pre_scattered[:, keys : 2 * keys],
        pre_scattered[:, 2 * keys :],
        side_scattered[:, vals:],
        down_scattered,
        decay_up_grad,
        decay_bias_grad,
        taps_grad[:, :keys],
        taps_grad[:, keys : 2 * keys],
        taps_grad[:, 2 * keys :],
        group_gain_grad,
        side_scattered[:, :vals].T,
        norms[1],
        feed_scattered[:, :hidden].astype(f32),
        feed_scattered[:, padded : padded + hidden].astype(f32),
        feed_scattered[:, 2 * padded : 2 * padded + hidden].astype(f32).T,
    )


def total_latent(parts):
    far = swap(parts[3], "head", 1)
    far = swap(parts[2] + far, "head", 2)
    near = swap(parts[1], "head", 1)
    return parts[0] + near + far


def solution(mesh):
    placed = (
        P(None, "seq", None),
        P(None, "seq", None),
        P(),
        P(None, "head"),
        P(None, "head"),
        P(None, "head"),
        P(None, "head"),
        P(),
        P(None, "head"),
        P("head"),
        P(None, "head"),
        P(None, "head"),
        P(None, "head"),
        P("head"),
        P("head", None),
        P(),
        P(None, "head"),
        P(None, "head"),
        P("head", None),
    )
    return jax.shard_map(
        shards,
        mesh=mesh,
        in_specs=placed,
        out_specs=(
            P(None, "seq", None),
            P(None, "seq", None),
            P(),
            P("seq", "head"),
            P("seq", "head"),
            P("seq", "head"),
            P("seq", "head"),
            P("seq", None),
            P(None, "head"),
            P("head"),
            P(None, "head"),
            P(None, "head"),
            P(None, "head"),
            P("head"),
            P("head", "seq"),
            P(),
            P("seq", "head"),
            P("seq", "head"),
            P("head", "seq"),
        ),
        check_vma=False,
    )
```

```python
import functools

import functools

import jax
import jax.numpy as jnp
from jax import lax
from jax.experimental import pallas as pl
from jax.experimental.pallas import tpu as pltpu
from jax.sharding import PartitionSpec as P

KH = 128
VH = 256
STRETCH = 64
CONV = 4
SCALE = KH**-0.5
PAD = 8

epsilon = 1e-06
highest = lax.Precision.HIGHEST
f32 = jnp.float32
bf16 = jnp.bfloat16
VMEM = 50 * 1024 * 1024


def dot(a, b, dims=((1,), (0,)), precision=None):
    return lax.dot_general(a, b, (dims, ((), ())), precision=precision, preferred_element_type=f32)


NT = ((1,), (1,))
TN = ((0,), (0,))


def split_dot(left, values, dims=((1,), (0,))):
    high = values.astype(bf16)
    low = (values - high.astype(f32)).astype(bf16)
    return dot(left, high, dims) + dot(left, low, dims)


def two_pieces(values):
    high = values.astype(bf16)
    return high, (values - high.astype(f32)).astype(bf16)


def lower(span, strict=False):
    row = lax.broadcasted_iota(jnp.int32, (span, span), 0)
    col = lax.broadcasted_iota(jnp.int32, (span, span), 1)
    return (row > col) if strict else (row >= col)


def as_bf(mask):
    return jnp.where(mask, 1.0, 0.0).astype(bf16)


def call(body, grid, ins, outs, scratch=(), order=None, after=(), into=()):
    lead = [] if order is None else [order]
    arrays = lead + [entry[0] for entry in ins] + list(after) + list(into)
    in_specs = [
        pl.BlockSpec(memory_space=pltpu.SMEM) if entry[1] is None else pl.BlockSpec(entry[1], entry[2])
        for entry in ins
    ]
    in_specs += [pl.BlockSpec(memory_space=pl.ANY)] * (len(after) + len(into))
    first, skip = len(lead) + len(ins), len(after) + len(into)

    def run(*refs):
        body(*refs[len(lead) : first], *refs[first + skip :])

    return pl.pallas_call(
        run,
        out_shape=[jax.ShapeDtypeStruct(entry[0], entry[1]) for entry in outs],
        grid_spec=pltpu.PrefetchScalarGridSpec(
            num_scalar_prefetch=len(lead),
            grid=grid,
            in_specs=in_specs,
            out_specs=[pl.BlockSpec(entry[2], entry[3]) for entry in outs],
            scratch_shapes=list(scratch),
        ),
        input_output_aliases={first + len(after) + k: k for k in range(len(into))},
        compiler_params=pltpu.CompilerParams(vmem_limit_bytes=VMEM),
        cost_estimate=pl.CostEstimate(flops=1, bytes_accessed=1, transcendentals=0),
    )(*arrays)


def held(array, after):
    def body(*refs):
        pass

    return pl.pallas_call(
        body,
        out_shape=jax.ShapeDtypeStruct(array.shape, array.dtype),
        in_specs=[pl.BlockSpec(memory_space=pl.ANY)] * (1 + len(after)),
        out_specs=pl.BlockSpec(memory_space=pl.ANY),
        input_output_aliases={0: 0},
        cost_estimate=pl.CostEstimate(flops=1, bytes_accessed=1, transcendentals=0),
    )(array, *after)


def whole(array):
    zeros = (0,) * array.ndim
    return (array, array.shape, lambda *_: zeros)


def by_slot(array, base=0):
    rest = (0,) * (array.ndim - 1)
    return (array, (None,) + array.shape[1:], lambda i, *_: (i + base,) + rest)


def at_slot(array, slot):
    rest = (0,) * (array.ndim - 1)
    return (array, (None,) + array.shape[1:], lambda *_: (slot,) + rest)


def out_by_slot(shape, dtype, base=0):
    rest = (0,) * (len(shape) - 1)
    return (shape, dtype, (None,) + shape[1:], lambda i, *_: (i + base,) + rest)


def out_at_slot(shape, dtype, slot):
    rest = (0,) * (len(shape) - 1)
    return (shape, dtype, (None,) + shape[1:], lambda *_: (slot,) + rest)


def out_whole(shape, dtype):
    zeros = (0,) * len(shape)
    return (shape, dtype, shape, lambda *_: zeros)


def project_body(tokens, gain, w_query, w_key, w_value, normed, pre):
    values = tokens[...].astype(f32)
    scaled = values * lax.rsqrt(jnp.mean(values * values, axis=-1, keepdims=True) + epsilon)
    low = (scaled * gain[...]).astype(bf16)
    normed[...] = low
    keys, vals = w_query.shape[1], w_value.shape[1]
    pre[:, :keys] = dot(low, w_query[...]).astype(bf16)
    pre[:, keys : 2 * keys] = dot(low, w_key[...]).astype(bf16)
    pre[:, 2 * keys :] = dot(low, w_value[...]).astype(bf16)


def gate_body(normed, w_gate, w_down, gate_pre, latent):
    low = normed[...]
    gate_pre[...] = dot(low, w_gate[...])
    latent[...] = dot(low, w_down[...])


def conv_sum(scratch, taps, rows):
    summed = taps[0:1, :] * scratch[pl.ds(PAD - CONV + 1, rows), :]
    for offset in range(1, CONV):
        summed = summed + taps[offset : offset + 1, :] * scratch[
            pl.ds(PAD - CONV + 1 + offset, rows), :
        ]
    return summed


def decay_logits(latent, up, bias):
    return dot(latent[...], up[...], precision=highest) + bias[...]


def conv_body(
    pre, halo, taps, latent, up, bias,
    queries, key_vecs, val_vecs, inner_sum, starts, states, state_out, edges, message, ext,
):
    rows = pre.shape[0]
    ext[0:PAD, :] = halo[...].astype(f32)
    ext[PAD : PAD + rows, :] = pre[...].astype(f32)
    summed = conv_sum(ext, taps[...], rows)
    active = (summed * jax.nn.sigmoid(summed)).astype(bf16)
    queries[...] = active[:, :KH]
    key_vecs[...] = active[:, KH : 2 * KH]
    val_vecs[...] = active[:, 2 * KH :]
    logits = decay_logits(latent, up, bias)
    logdec = (jnp.minimum(logits, 0.0) - jnp.log1p(jnp.exp(-jnp.abs(logits)))) * (1.0 / 16.0)
    tril = jnp.where(lower(STRETCH), 1.0, 0.0)
    state = jnp.zeros((VH, KH), f32)
    before = jnp.zeros((1, KH), f32)
    for block in range(rows // STRETCH):
        at = slice(block * STRETCH, (block + 1) * STRETCH)
        total = dot(tril, logdec[at], precision=highest)
        inner_sum[at, :] = total
        last = total[STRETCH - 1 : STRETCH]
        starts[block : block + 1, :] = before
        states[block] = state
        carried = (active[at, KH : 2 * KH].astype(f32) * jnp.exp(last - total)).astype(bf16)
        state = state * jnp.exp(last) + dot(active[at, 2 * KH :], carried, TN)
        before = before + last
    state_out[...] = state
    decay = jnp.exp(before)
    edges[...] = jnp.where(first_row((8, KH)), decay, 1.0)
    pack_state(state, decay, message)


def first_row(shape, row=0):
    return lax.broadcasted_iota(jnp.int32, shape, 0) == row


def guess(column, line):
    one = jnp.where(first_row((16, column.shape[1])), column, 0.0).astype(bf16)
    two = jnp.where(first_row((16, line.shape[1])), line, 0.0).astype(bf16)
    return dot(one, two, TN)


def pack_state(state, decay, message):
    line = jnp.mean(state, axis=0, keepdims=True).astype(bf16).astype(f32)
    size = jnp.maximum(jnp.sum(line * line, axis=1, keepdims=True), 1e-30)
    lines = jnp.broadcast_to(line, (16, KH)).astype(bf16)
    column = dot(lines, state.astype(bf16), NT)[0:1] / size
    column = column.astype(bf16).astype(f32)
    message[0:VH, :] = (state - guess(column, line)).astype(bf16)
    high, low = two_pieces(decay)
    edge = jnp.zeros((16, KH), f32)
    for row, value in enumerate(
        (high.astype(f32), low.astype(f32), line, column[:, :KH], column[:, KH:])
    ):
        edge = jnp.where(first_row((16, KH), row), value, edge)
    message[VH:, :] = edge.astype(bf16)


def unpack_state(message):
    edge = message[VH:, :].astype(f32)
    column = jnp.concatenate([edge[3:4], edge[4:5]], axis=1)
    return message[0:VH, :].astype(f32) + guess(column, edge[2:3]), edge[0:1] + edge[1:2]


def is_later(place, level):
    return lax.rem(lax.div(place[0], 1 << level), 2) == 1


def combine_body(level, place, state, edges, result, other, *outs):
    theirs, their_decay = unpack_state(other)
    is_upper = is_later(place, level)
    own_decay, passed = edges[0:1, :], edges[1:2, :]
    new_result, new_edges = outs[0], outs[1]
    new_result[...] = result[...] + jnp.where(is_upper, passed * theirs, 0.0)
    low_decay = jnp.where(is_upper, their_decay, own_decay)
    high_decay = jnp.where(is_upper, own_decay, their_decay)
    both = low_decay * high_decay
    after = jnp.where(is_upper, passed * their_decay, passed)
    edge = jnp.zeros((8, KH), f32)
    for row, value in enumerate((both, after, their_decay, own_decay)):
        edge = jnp.where(first_row((8, KH), row), value, edge)
    new_edges[...] = edge
    if len(outs) > 2:
        own = state[...]
        joined = high_decay * jnp.where(is_upper, theirs, own) + jnp.where(is_upper, own, theirs)
        outs[2][...] = joined
        pack_state(joined, both, outs[3])


def halves(total):
    middle = total[STRETCH // 2 - 1 : STRETCH // 2]
    return jnp.exp(total - middle), jnp.exp(middle - total)


def close_scores(mask, ahead, behind):
    total = dot(ahead[0], behind[0], NT) + (
        dot(ahead[0], behind[1], NT) + dot(ahead[1], behind[0], NT)
    )
    return jnp.where(mask, total, 0.0)


def local_body(queries, key_vecs, val_vecs, inner_sum, states, attended):
    mask = lower(STRETCH)
    for block in range(queries.shape[0] // STRETCH):
        at = slice(block * STRETCH, (block + 1) * STRETCH)
        total = inner_sum[at, :]
        query = queries[at, :].astype(f32) * SCALE
        up, down = halves(total)
        scores, score_rest = two_pieces(
            close_scores(
                mask, two_pieces(query * up), two_pieces(key_vecs[at, :].astype(f32) * down)
            )
        )
        entering, rest = two_pieces(query * jnp.exp(total))
        high, low = two_pieces(states[block])
        attended[at, :] = (
            dot(scores, val_vecs[at, :])
            + dot(score_rest, val_vecs[at, :])
            + dot(entering, high, NT)
            + dot(entering, low, NT)
            + dot(rest, high, NT)
        )


def device_sum(inner_sum, starts):
    rows = inner_sum.shape[0]
    return jnp.concatenate(
        [
            inner_sum[block * STRETCH : (block + 1) * STRETCH, :] + starts[block : block + 1, :]
            for block in range(rows // STRETCH)
        ],
        axis=0,
    )


def mix_body(
    local, queries, inner_sum, starts, incoming, gate_pre, gain, w_out, *rest_refs
):
    attended, gated, mixed = rest_refs[-3:]
    total = device_sum(inner_sum, starts)
    entering, rest = two_pieces(queries[...].astype(f32) * SCALE * jnp.exp(total))
    high, low = two_pieces(incoming[...])
    values = local[...] + dot(entering, high, NT) + dot(entering, low, NT) + dot(rest, high, NT)
    attended[...] = values
    scaled = values * lax.rsqrt(jnp.mean(values * values, axis=-1, keepdims=True) + epsilon)
    gate = gate_pre[...]
    low = (scaled * gain[...] * (gate * jax.nn.sigmoid(gate))).astype(bf16)
    gated[...] = low
    summed = dot(low, w_out[...])
    if len(rest_refs) > 3:
        summed = summed + rest_refs[0][...].astype(f32)
    mixed[...] = summed.astype(mixed.dtype)


def restore_body(one, two, out):
    @pl.when(pl.program_id(0) == 0)
    def _():
        out[...] = one[...].astype(out.dtype)

    @pl.when(pl.program_id(0) == 1)
    def _():
        out[...] = two[...].astype(out.dtype)


def share_body(tokens, parts, near, far, gain, hidden, second):
    values = (
        tokens[...].astype(f32) + parts[...] + near[...].astype(f32) + far[...].astype(f32)
    )
    hidden[...] = values
    scaled = values * lax.rsqrt(jnp.mean(values * values, axis=-1, keepdims=True) + epsilon)
    second[...] = (scaled * gain[...]).astype(bf16)


def add_gain(out, first, values):
    @pl.when(pl.program_id(0) == 0)
    def _():
        out[first : first + values.shape[1] // KH, :] = jnp.zeros((values.shape[1] // KH, KH), f32)

    part = jnp.sum(values, axis=0, keepdims=True)
    for piece in range(values.shape[1] // KH):
        out[first + piece : first + piece + 1, :] += part[:, piece * KH : (piece + 1) * KH]


def share_back_body(hidden, cotangent, parts, near, far, gain, grad_hidden, low, gain_part):
    grad = parts[...] + near[...].astype(f32) + far[...].astype(f32)
    values = hidden[...]
    inverse = lax.rsqrt(jnp.mean(values * values, axis=-1, keepdims=True) + epsilon)
    scaled = values * inverse
    add_gain(gain_part, 0, grad * scaled)
    inner = grad * gain[...]
    inner = inverse * (inner - scaled * jnp.mean(inner * scaled, axis=-1, keepdims=True))
    total = cotangent[...].astype(f32) + inner
    grad_hidden[...] = total
    low[...] = total.astype(bf16)


def sum_body(one, two, out):
    out[...] = (one[...] + two[...]).astype(out.dtype)


def join_body(one, two, out):
    out[...] = (one[...] + two[...].astype(f32)).astype(out.dtype)


def layer_body(hidden, parts, near, far, out):
    total = hidden[...] + parts[...] + near[...].astype(f32) + far[...].astype(f32)
    out[...] = total.astype(out.dtype)


def feed_body(
    normed, cotangent, w_gate, w_up, w_down, inner, grad_gate, grad_up, grad_normed, feed_out
):
    low = normed[...]
    gate = dot(low, w_gate[...])
    up = dot(low, w_up[...])
    grad = dot(cotangent[...], w_down[...], NT)
    soft = jax.nn.sigmoid(gate)
    silu = gate * soft
    product = (silu * up).astype(bf16)
    inner[...] = product
    gate_low = (grad * up * (soft * (1.0 + gate * (1.0 - soft)))).astype(bf16)
    up_low = (grad * silu).astype(bf16)
    grad_gate[...] = gate_low
    grad_up[...] = up_low
    feed_out[...] = dot(product, w_down[...]).astype(feed_out.dtype)
    summed = dot(gate_low, w_gate[...], NT) + dot(up_low, w_up[...], NT)
    grad_normed[...] = summed.astype(grad_normed.dtype)


def gate_back_body(
    grad_hidden, w_out, attended, gate_pre, gain, queries, inner_sum, starts,
    grad_attended, grad_gate, state, gain_part,
):
    grad = dot(grad_hidden[...], w_out[...], NT)
    values = attended[...]
    inverse = lax.rsqrt(jnp.mean(values * values, axis=-1, keepdims=True) + epsilon)
    scaled = values * inverse
    gate = gate_pre[...]
    soft = jax.nn.sigmoid(gate)
    grad_gate[...] = (
        grad * scaled * gain[...] * (soft * (1.0 + gate * (1.0 - soft)))
    ).astype(bf16)
    grad = grad * (gate * soft)
    gain_part[...] = jnp.broadcast_to(jnp.sum(grad * scaled, axis=0, keepdims=True), gain_part.shape)
    grad = grad * gain[...]
    grad = inverse * (grad - scaled * jnp.mean(grad * scaled, axis=-1, keepdims=True))
    grad_attended[...] = grad
    high, low = two_pieces(grad)
    total = device_sum(inner_sum, starts)
    entering = (queries[...].astype(f32) * SCALE * jnp.exp(total)).astype(bf16)
    summed = dot(high, entering, TN) + dot(low, entering, TN)
    state[...] = summed


def local_back_body(
    queries, key_vecs, val_vecs, inner_sum, starts, states, incoming, grad_attended,
    grad_queries, grad_keys, grad_vals, grad_logdec,
):
    mask = lower(STRETCH)
    row = lax.broadcasted_iota(jnp.int32, (STRETCH, 2 * STRETCH), 0)
    col = lax.broadcasted_iota(jnp.int32, (STRETCH, 2 * STRETCH), 1)
    later = jnp.where(col >= row, 1.0, 0.0)
    earlier = jnp.where(col - STRETCH < row, 1.0, 0.0)
    sums = jnp.where(col < STRETCH, later, earlier).astype(bf16)
    running = jnp.zeros((VH, KH), f32)
    entered = incoming[...]
    for block in reversed(range(queries.shape[0] // STRETCH)):
        at = slice(block * STRETCH, (block + 1) * STRETCH)
        total = inner_sum[at, :]
        last = total[STRETCH - 1 : STRETCH]
        query = queries[at, :].astype(f32) * SCALE
        key = key_vecs[at, :].astype(f32)
        val = val_vecs[at, :]
        grad, grad_rest = two_pieces(grad_attended[at, :])
        up, down = halves(total)
        whole_up = jnp.exp(total)
        rest = jnp.exp(last - total)
        ahead, ahead_rest = two_pieces(query * up)
        behind, behind_rest = two_pieces(key * down)
        entering = (query * whole_up).astype(bf16)
        carried = (key * rest).astype(bf16)
        current = states[block] + entered * jnp.exp(starts[block : block + 1, :])
        scores = close_scores(mask, (ahead, ahead_rest), (behind, behind_rest)).astype(bf16)
        grad_scores = jnp.where(mask, dot(grad, val, NT) + dot(grad_rest, val, NT), 0.0).astype(bf16)
        running_low, running_rest = two_pieces(running)
        current_low, current_rest = two_pieces(current)
        grad_ahead = dot(grad_scores, behind)
        grad_behind = dot(grad_scores, ahead, TN)
        grad_entering = (
            dot(grad, current_low) + dot(grad, current_rest) + dot(grad_rest, current_low)
        )
        grad_carried = dot(val, running_low) + dot(val, running_rest)
        grad_vals[at, :] = dot(scores, grad, TN) + dot(carried, running_low, NT)
        grad_queries[at, :] = (grad_ahead * up + grad_entering * whole_up) * SCALE
        grad_keys[at, :] = grad_behind * down + grad_carried * rest
        inside = (
            ahead.astype(f32) * grad_ahead
            - behind.astype(f32) * grad_behind
            + entering.astype(f32) * grad_entering
        )
        stacked = jnp.concatenate([inside, carried.astype(f32) * grad_carried], axis=0)
        through = jnp.sum(current * running, axis=0, keepdims=True) * jnp.exp(last)
        grad_logdec[at, :] = split_dot(sums, stacked) + through
        running = running * jnp.exp(last) + dot(grad, entering, TN) + dot(grad_rest, entering, TN)


def conv_back_body(
    grad_queries, grad_keys, grad_vals, grad_logdec, key_vecs, val_vecs, inner_sum, starts,
    incoming, outgoing, pre, halo, taps, latent, up, bias,
    gain_zero, gain_one, gain_two, gain_three,
    grad_pre, tail, head, grad_latent, small, ext, back,
):
    rows = pre.shape[0]
    keys = grad_queries.shape[1]
    ext[0:PAD, :] = halo[...].astype(f32)
    ext[PAD : PAD + rows, :] = pre[...].astype(f32)
    summed = conv_sum(ext, taps[...], rows)
    soft = jax.nn.sigmoid(summed)
    slope = soft * (1.0 + summed * (1.0 - soft))
    total = device_sum(inner_sum, starts)
    final = total[rows - 1 : rows]
    rest = jnp.exp(final - total)
    leaving, leaving_rest = two_pieces(outgoing[...])
    carried = (key_vecs[...].astype(f32) * rest).astype(bf16)
    grad_carried = dot(val_vecs[...], leaving) + dot(val_vecs[...], leaving_rest)
    back[0:PAD, :] = jnp.zeros((PAD, back.shape[1]), f32)
    back[PAD + rows :, :] = jnp.zeros((PAD, back.shape[1]), f32)
    back[PAD : PAD + rows, 0:keys] = grad_queries[...] * slope[:, 0:keys]
    back[PAD : PAD + rows, keys : 2 * keys] = (grad_keys[...] + grad_carried * rest) * slope[
        :, keys : 2 * keys
    ]
    back[PAD : PAD + rows, 2 * keys :] = (grad_vals[...] + dot(carried, leaving, NT)) * slope[
        :, 2 * keys :
    ]
    pairs = carried.astype(f32) * grad_carried
    strict = as_bf(lower(STRETCH, True))
    through = jnp.sum(incoming[...] * outgoing[...], axis=0, keepdims=True) * jnp.exp(final)
    logits = decay_logits(latent, up, bias)
    fade = jax.nn.sigmoid(-logits) * (1.0 / 16.0)
    pieces = []
    for block in range(rows // STRETCH):
        at = slice(block * STRETCH, (block + 1) * STRETCH)
        pieces.append(grad_logdec[at, :] + split_dot(strict, pairs[at]) + through)
        through = through + jnp.sum(pairs[at], axis=0, keepdims=True)
    grad_logits = jnp.concatenate(pieces, axis=0) * fade
    gains = gain_zero[0:1, :] + gain_one[0:1, :] + gain_two[0:1, :] + gain_three[0:1, :]

    @pl.when(pl.program_id(0) == 0)
    def _():
        small[...] = jnp.zeros(small.shape, f32)
        small[0:1, :] = gains[:, :KH]
        small[1:2, :] = gains[:, KH:]

    small[2:3, :] += jnp.sum(grad_logits, axis=0, keepdims=True)
    rank = latent.shape[1]
    small[8 : 8 + rank, :] += dot(latent[...], grad_logits, TN, highest)
    grad_latent[...] = dot(up[...], grad_logits, NT, highest)
    kernel = taps[...]
    grad = kernel[0:1, :] * back[pl.ds(CONV - 1, PAD + rows), :]
    for offset in range(1, CONV):
        grad = grad + kernel[offset : offset + 1, :] * back[
            pl.ds(CONV - 1 - offset, PAD + rows), :
        ]
    head[...] = grad[0:PAD]
    tail[...] = grad[rows:]
    grad_pre[...] = grad[PAD:].astype(bf16)
    inner = back[PAD : PAD + rows, :]
    for offset in range(CONV):
        part = jnp.sum(
            inner * ext[pl.ds(PAD - CONV + 1 + offset, rows), :], axis=0, keepdims=True
        )
        for piece in range(part.shape[1] // KH):
            row = 8 + rank + offset * (part.shape[1] // KH) + piece
            small[row : row + 1, :] += part[:, piece * KH : (piece + 1) * KH]


def project_back_body(
    grad_pre, tail, arrived, grad_gate, w_query, w_key, w_value, w_gate, *rest_refs
):
    fixed, grad_normed = rest_refs[-2:]
    rows = grad_pre.shape[0]
    keys = w_query.shape[1]
    fixed[0 : rows - 16, :] = grad_pre[0 : rows - 16, :]
    ending = jnp.concatenate(
        [grad_pre[rows - 16 : rows, :].astype(f32)[0 : 16 - PAD], tail[...] + arrived[...]], axis=0
    )
    fixed[rows - 16 : rows, :] = ending.astype(bf16)
    low = fixed[...]
    summed = dot(low[:, 0:keys], w_query[...], NT) + dot(low[:, keys : 2 * keys], w_key[...], NT)
    summed = summed + dot(low[:, 2 * keys :], w_value[...], NT)
    summed = summed + dot(grad_gate[...], w_gate[...], NT)
    if len(rest_refs) > 2:
        summed = summed + rest_refs[0][...].astype(f32)
    grad_normed[...] = summed.astype(grad_normed.dtype)


def first_back_body(
    tokens, grad_hidden, parts, near, far, latent, w_down, gain, others, small, token_grad, sums
):
    grad = parts[...] + near[...].astype(f32) + far[...].astype(f32)
    grad = grad + dot(latent[...], w_down[...], ((0,), (1,)))
    values = tokens[...].astype(f32)
    inverse = lax.rsqrt(jnp.mean(values * values, axis=-1, keepdims=True) + epsilon)
    scaled = values * inverse
    count = others.shape[0]
    add_gain(sums, 0, grad * scaled)
    sums[count : 2 * count, :] = others[...]
    sums[2 * count :, :] = small[...]
    inner = grad * gain[...]
    inner = inverse * (inner - scaled * jnp.mean(inner * scaled, axis=-1, keepdims=True))
    token_grad[...] = (grad_hidden[...] + inner).astype(bf16)


def weight_grads(jobs, width, order=None, after=(), latent=None, blocks=4):
    arrays, plan, ins = [], [], []
    depth = width_of = None
    for left, right, first in jobs:
        entry = []
        for side, group in ((0, left), (1, right)):
            places = []
            if side == 0 and not isinstance(group, list) and order is not None and latent is None:
                group = [(group, slot) for slot in range(group.shape[0])]
            for item in group if isinstance(group, list) else [group]:
                array, slot = item if isinstance(item, tuple) else (item, None)
                known = [k for k, a in enumerate(arrays) if a[0] is array and a[1:] == (side, slot)]
                if not known:
                    arrays.append((array, side, slot))
                    known = [len(arrays) - 1]
                places.append(known[0])
            entry.append(places)
        plan.append((entry[0], entry[1], first))
    depth = arrays[0][0].shape[-1]
    block = depth // blocks
    for array, side, slot in arrays:
        if side == 1:
            ins.append(whole(array))
        elif slot is not None:
            ins.append(
                (
                    array,
                    (None, array.shape[1], block),
                    functools.partial(lambda k, i, ref: (ref[k], 0, i), slot),
                )
            )
        elif array.ndim == 2:
            ins.append((array, (array.shape[0], block), lambda i, *_: (0, i)))
        else:
            ins.append((array, array.shape[:2] + (block,), lambda i, *_: (0, 0, i)))
    if latent is not None:
        ins.append((order, None, None))
        ins.append(whole(latent))

    def body(*refs):
        out = refs[len(ins)]
        covered = 0
        for lefts, rights, first in plan:
            total = None
            pairs = []
            for left, right in zip(lefts, rights):
                a, b = refs[left], refs[right]
                if len(a.shape) == 2:
                    pairs.append((a, b))
                else:
                    pairs += [(a.at[k], b.at[k]) for k in range(a.shape[0])]
            for one, two in pairs:
                term = dot(one[...], two[...], TN)
                total = term if total is None else total + term
            if first > covered:
                out[:, covered:first] = jnp.zeros((block, first - covered), bf16)
            out[:, first : first + total.shape[1]] = total.astype(bf16)
            covered = first + total.shape[1]
        if covered < width:
            out[:, covered:] = jnp.zeros((block, width - covered), bf16)
        if latent is not None:
            place, factor, parts = refs[len(ins) - 2], refs[len(ins) - 1], refs[len(ins) + 1]
            one = refs[plan[0][0][0]]
            for slot in range(factor.shape[0]):
                parts[place[slot]] = dot(one[slot], factor[slot], ((0,), (1,)))
            total = parts[0]
            for sequence in range(1, factor.shape[0]):
                total = total + parts[sequence]
            out[:, covered : covered + total.shape[1]] = total.astype(bf16)

    return call(
        body,
        (blocks,),
        ins,
        [((depth, width), bf16, (block, width), lambda i, *_: (i, 0))],
        [] if latent is None else [pltpu.VMEM((latent.shape[0], block, latent.shape[1]), f32)],
        order=order if latent is None else None,
        after=after,
    )[0]


def bits_of(axis):
    count = lax.axis_size(axis)
    return [1 << k for k in range(count.bit_length() - 1)]


def swap(value, axis, bit):
    count = lax.axis_size(axis)
    return lax.ppermute(value, axis, [(source, source ^ bit) for source in range(count)])


def passed_along(value, axis, steps):
    count = lax.axis_size(axis)
    first, last = (max(0, -steps), min(count, count - steps))
    return lax.ppermute(value, axis, [(source, source + steps) for source in range(first, last)])


def combine_back_body(level, place, state, edges, behind, result, other, *outs):
    theirs = other[...]
    is_upper = is_later(place, level)
    their_decay, own_decay = edges[2:3, :], edges[3:4, :]
    passed = behind[0:1, :]
    outs[0][...] = result[...] + jnp.where(is_upper, 0.0, passed * theirs)
    outs[1][...] = jnp.broadcast_to(jnp.where(is_upper, passed, passed * their_decay), behind.shape)
    if len(outs) > 2:
        own = state[...]
        low_decay = jnp.where(is_upper, their_decay, own_decay)
        joined = jnp.where(is_upper, theirs, own) + low_decay * jnp.where(is_upper, own, theirs)
        outs[2][...] = joined


def entering_states(place, state, edges, message, fillers):
    slots = state.shape[0]
    result = jnp.zeros_like(state)
    kept = []
    bits = bits_of("seq")
    for level, bit in enumerate(bits):
        other = swap(message, "seq", bit)
        beside = fillers[level](message) if level < len(fillers) else ()
        last = level + 1 == len(bits)
        outs = [out_by_slot((slots, VH, KH), f32), out_by_slot((slots, 8, KH), f32)]
        if not last:
            outs += [out_by_slot((slots, VH, KH), f32), out_by_slot((slots, VH + 16, KH), bf16)]
        given = call(
            functools.partial(combine_body, level),
            (slots,),
            [place] + [by_slot(a) for a in (state, edges, result, other)],
            outs,
            after=beside,
        )
        result, edges = given[0], given[1]
        kept.append(edges)
        if not last:
            state, message = given[2], given[3]
    return result, kept


def leaving_states(place, state, kept, fillers):
    slots = state.shape[0]
    result = jnp.zeros_like(state)
    behind = jnp.ones((slots, 8, KH), f32)
    bits = bits_of("seq")
    for level, bit in enumerate(bits):
        other = swap(state, "seq", bit)
        beside = fillers[level](state) if level < len(fillers) else ()
        last = level + 1 == len(bits)
        outs = [out_by_slot((slots, VH, KH), f32), out_by_slot((slots, 8, KH), f32)]
        if not last:
            outs += [out_by_slot((slots, VH, KH), f32)]
        given = call(
            functools.partial(combine_back_body, level),
            (slots,),
            [place] + [by_slot(a) for a in (state, kept[level], behind, result, other)],
            outs,
            after=beside,
        )
        result, behind = given[0], given[1]
        if not last:
            state = given[2]
    return result


def total_sum(value, axes):
    for axis in axes:
        for bit in bits_of(axis):
            value = value + swap(value, axis, bit)
    return value


def scatter_sum(value, axis, after):
    place = lax.axis_index(axis).astype(jnp.uint32)
    parts = lax.axis_size(axis)
    columns = value.shape[1]
    block = value.shape[0] // parts
    current = value
    for level, bit in enumerate(bits_of(axis)):
        if level < len(after) and after[level]:
            current = held(current, after[level])
        mine = (place // bit) % 2
        pairs = current.reshape(parts // (2 * bit), 2, block, columns)
        zero = jnp.uint32(0)
        shape = (parts // (2 * bit), 1, block, columns)
        kept = lax.dynamic_slice(pairs, (zero, mine, zero, zero), shape)
        sent = lax.dynamic_slice(pairs, (zero, 1 - mine, zero, zero), shape)
        got = swap(sent.astype(bf16), axis, bit)
        current = kept.astype(f32) + got.astype(f32)
        if 2 * bit < parts:
            current = current.astype(bf16)
    return current.reshape(block, columns)


def gather_slots(own):
    one = swap(own, "head", 1)
    two = swap(own, "head", 2)
    three = swap(two, "head", 1)
    return [own, one, two, three]


RING = (3, 1, 2, 0)


def shards(
    tokens,
    cotangent,
    mixer_norm,
    query_weight,
    key_weight,
    value_weight,
    gate_weight,
    decay_down,
    decay_up,
    decay_bias,
    query_conv,
    key_conv,
    value_conv,
    group_gain,
    output_weight,
    feed_norm,
    feed_gate,
    feed_up,
    feed_down,
):
    slots, rows, width = tokens.shape
    keys = query_weight.shape[1]
    vals = value_weight.shape[1]
    hidden = feed_gate.shape[1]
    rank = decay_down.shape[1]
    all_cols = 2 * keys + vals
    blocks = rows // STRETCH
    assert slots == lax.axis_size("head") == 4 and keys == KH and vals == VH
    me = lax.axis_index("head")
    place = lax.axis_index("seq").astype(jnp.int32).reshape(1)
    place = (place, None, None)
    order = jnp.bitwise_xor(jnp.arange(slots, dtype=jnp.int32), me.astype(jnp.int32))

    tile = min(256, rows)
    count = rows // tile
    rowed = lambda i, *_: (i, 0)

    def tiles(*arrays):
        return [(array, (tile, array.shape[1]), rowed) for array in arrays]

    def sequence(array, slot):
        return (array, (None, tile, width), lambda i, order_ref: (order_ref[slot], i, 0))

    def restored(base, one, two, dtype, into=(), after=()):
        return call(
            restore_body,
            (2, count),
            [
                (one, (tile, width), lambda s, i, *_: (jnp.where(s == 0, i, count - 1), 0)),
                (two, (tile, width), lambda s, i, *_: (jnp.where(s == 1, i, 0), 0)),
            ],
            [
                (
                    (slots, rows, width),
                    dtype,
                    (None, tile, width),
                    lambda s, i, order_ref: (order_ref[base + s], i, 0),
                )
            ],
            order=order,
            after=after,
            into=into,
        )

    taps = jnp.concatenate([query_conv, key_conv, value_conv], axis=-1)
    gain_row = group_gain.reshape(1, vals)
    bias_row = decay_bias.reshape(1, keys)

    normed, pre = call(
        project_body,
        (slots,),
        [
            (tokens, (None, rows, width), lambda i, order_ref: (order_ref[i], 0, 0)),
            whole(mixer_norm.reshape(1, width)),
            whole(query_weight),
            whole(key_weight),
            whole(value_weight),
        ],
        [
            out_by_slot((slots, rows, width), bf16),
            out_by_slot((slots, rows, all_cols), bf16),
        ],
        order=order,
    )
    halo = passed_along(pre[:, rows - PAD :, :], "seq", 1)
    gate_pre, latent = call(
        gate_body,
        (slots,),
        [by_slot(normed), whole(gate_weight), whole(decay_down)],
        [
            out_by_slot((slots, rows, vals), f32),
            out_by_slot((slots, rows, rank), f32),
        ],
    )
    queries, key_vecs, val_vecs, inner_sum, starts, states, total, edges, message = call(
        conv_body,
        (slots,),
        [
            by_slot(pre),
            by_slot(halo),
            whole(taps),
            by_slot(latent),
            whole(decay_up),
            whole(bias_row),
        ],
        [
            out_by_slot((slots, rows, keys), bf16),
            out_by_slot((slots, rows, keys), bf16),
            out_by_slot((slots, rows, vals), bf16),
            out_by_slot((slots, rows, keys), f32),
            out_by_slot((slots, blocks, keys), f32),
            out_by_slot((slots, blocks, VH, KH), f32),
            out_by_slot((slots, VH, KH), f32),
            out_by_slot((slots, 8, KH), f32),
            out_by_slot((slots, VH + 16, KH), bf16),
        ],
        [pltpu.VMEM((PAD + rows, all_cols), f32)],
    )
    local = ()

    def local_part(base):
        def make(message):
            nonlocal local
            local = call(
                local_body,
                (2,),
                [by_slot(a, base) for a in (queries, key_vecs, val_vecs, inner_sum, states)],
                [out_by_slot((slots, rows, vals), f32, base)],
                after=(message,),
                into=local,
            )
            return tuple(local)

        return make

    incoming, kept = entering_states(
        place,
        total,
        edges,
        message,
        [local_part(0), local_part(2), lambda message: (feed_gate, feed_up)],
    )
    local = local[0]

    attended, gated, mixed = [None] * 4, [None] * 4, [None] * 4
    done = ()
    far = None
    for slot in RING:
        extra = [whole(far)] if slot == 2 else []
        attended[slot], gated[slot], mixed[slot] = call(
            mix_body,
            (1,),
            [at_slot(a, slot) for a in (local, queries, inner_sum, starts, incoming, gate_pre)]
            + [whole(gain_row), whole(output_weight)]
            + extra,
            [
                out_whole((rows, vals), f32),
                out_whole((rows, vals), bf16),
                out_whole((rows, width), f32 if slot == 0 else bf16),
            ],
            after=done,
        )
        done = (mixed[slot],)
        if slot == 3:
            far = swap(mixed[3], "head", 1)
    near = swap(mixed[1], "head", 1)
    far = swap(mixed[2], "head", 2)
    norm_row = feed_norm.reshape(1, width)
    hidden_share, second = call(
        share_body,
        (rows // tile,),
        [sequence(tokens, 0)] + tiles(mixed[0], near, far) + [whole(norm_row)],
        [((rows, width), f32, (tile, width), rowed), ((rows, width), bf16, (tile, width), rowed)],
        order=order,
    )
    one, two = swap(second, "head", 1), swap(second, "head", 2)
    second_all = [second, one, None, None]

    inner, grad_gates, grad_ups, grad_seconds, feed_outs = ([None] * 4 for _ in range(5))
    done = ()
    for slot in (0, 1, 2, 3):
        wide = bf16 if slot % 2 else f32
        if slot == 2:
            second_all[2] = held(two, done)
            second_all[3] = swap(second_all[2], "head", 1)
        inner[slot], grad_gates[slot], grad_ups[slot], grad_seconds[slot], feed_outs[slot] = call(
            feed_body,
            (rows // tile,),
            tiles(second_all[slot])
            + [sequence(cotangent, slot)]
            + [whole(feed_gate), whole(feed_up), whole(feed_down)],
            [
                ((rows, hidden), bf16, (tile, hidden), rowed),
                ((rows, hidden), bf16, (tile, hidden), rowed),
                ((rows, hidden), bf16, (tile, hidden), rowed),
                ((rows, width), wide, (tile, width), rowed),
                ((rows, width), wide, (tile, width), rowed),
            ],
            order=order,
            after=done,
        )
        done = (inner[slot],)
    near = swap(grad_seconds[1], "head", 1)
    far = swap(grad_seconds[3], "head", 1)
    (joined,) = call(
        join_body,
        (count,),
        tiles(grad_seconds[2], far),
        [((rows, width), bf16, (tile, width), rowed)],
    )
    far = swap(joined, "head", 2)
    padded = -(-hidden // 128) * 128
    feed_pack = weight_grads(
        [
            (second_all, grad_gates, 0),
            (second_all, grad_ups, padded),
            (cotangent, inner, 2 * padded),
        ],
        3 * padded,
        order,
        (joined,),
    )
    grad_hidden_share, grad_hidden_low, feed_norm_part = call(
        share_back_body,
        (rows // tile,),
        tiles(hidden_share)
        + [sequence(cotangent, 0)]
        + tiles(grad_seconds[0], near, far)
        + [whole(norm_row)],
        [
            ((rows, width), f32, (tile, width), rowed),
            ((rows, width), bf16, (tile, width), rowed),
            out_whole((width // KH, KH), f32),
        ],
        order=order,
        after=(feed_pack,),
    )
    feed_scattered = lax.psum_scatter(
        held(feed_pack, (grad_hidden_low,)), "seq", scatter_dimension=0, tiled=True
    )
    one, two = swap(grad_hidden_low, "head", 1), swap(grad_hidden_low, "head", 2)
    grad_low = [grad_hidden_low, one, None, None]

    stacks, gain_parts = (), [None] * 4
    for slot in (0, 1, 2, 3):
        if slot == 2:
            grad_low[2] = held(two, stacks[:1])
            grad_low[3] = swap(grad_low[2], "head", 1)
        *stacks, gain_parts[slot] = call(
            gate_back_body,
            (1,),
            [whole(grad_low[slot]), whole(output_weight), whole(attended[slot])]
            + [at_slot(gate_pre, slot), whole(gain_row)]
            + [at_slot(a, slot) for a in (queries, inner_sum, starts)],
            [
                out_at_slot((slots, rows, vals), f32, slot),
                out_at_slot((slots, rows, vals), bf16, slot),
                out_at_slot((slots, VH, KH), f32, slot),
                out_whole((8, vals), f32),
            ],
            into=stacks,
        )
    grad_attended, grad_gate, back_state = stacks

    feed_far = swap(held(feed_outs[3], (back_state,)), "head", 1)
    feed_near = swap(feed_outs[1], "head", 1)

    def layer_sum(message):
        nonlocal feed_far
        (joined,) = call(
            join_body,
            (count,),
            tiles(feed_outs[2], feed_far),
            [((rows, width), bf16, (tile, width), rowed)],
        )
        feed_far = swap(joined, "head", 2)
        return (joined,)

    grad_local = ()

    def back_part(base):
        def make(message):
            nonlocal grad_local
            grad_local = call(
                local_back_body,
                (2,),
                [
                    by_slot(a, base)
                    for a in (
                        queries, key_vecs, val_vecs, inner_sum, starts, states, incoming, grad_attended,
                    )
                ],
                [
                    out_by_slot((slots, rows, keys), f32, base),
                    out_by_slot((slots, rows, keys), f32, base),
                    out_by_slot((slots, rows, vals), f32, base),
                    out_by_slot((slots, rows, keys), f32, base),
                ],
                after=(message,) + (layer_sum(message) if base == 0 else ()),
                into=grad_local,
            )
            return (grad_local[0],)

        return make

    def side_part(message):
        nonlocal side_pack
        side_pack = weight_grads(
            [(grad_low, gated, 0), (normed, grad_gate, vals)], 2 * vals, None, (message,)
        )
        return (side_pack,)

    side_pack = None
    outgoing = leaving_states(
        place, back_state, kept, [back_part(0), back_part(2), side_part]
    )
    side_scattered = lax.psum_scatter(
        held(side_pack, (outgoing, feed_scattered)), "seq", scatter_dimension=0, tiled=True
    )
    (layer_share,) = call(
        layer_body,
        (count,),
        tiles(hidden_share, feed_outs[0], feed_near, feed_far),
        [((rows, width), bf16, (tile, width), rowed)],
        after=(outgoing,),
    )
    layer_one, layer_two = swap(layer_share, "head", 1), swap(layer_share, "head", 2)
    small_rows = 8 + rank + CONV * all_cols // KH
    grad_pre, tail, head, grad_latent, small = call(
        conv_back_body,
        (slots,),
        [by_slot(a) for a in grad_local]
        + [by_slot(a) for a in (key_vecs, val_vecs, inner_sum, starts, incoming, outgoing)]
        + [by_slot(pre), by_slot(halo), whole(taps), by_slot(latent), whole(decay_up)]
        + [whole(bias_row)]
        + [whole(part) for part in gain_parts],
        [
            out_by_slot((slots, rows, all_cols), bf16),
            out_by_slot((slots, PAD, all_cols), f32),
            out_by_slot((slots, PAD, all_cols), f32),
            out_by_slot((slots, rank, rows), f32),
            out_whole((small_rows, KH), f32),
        ],
        [
            pltpu.VMEM((PAD + rows, all_cols), f32),
            pltpu.VMEM((2 * PAD + rows, all_cols), f32),
        ],
        after=(layer_share,),
    )
    arrived = passed_along(head, "seq", -1)
    layer_two = held(layer_two, (grad_pre,))
    layer_three = swap(layer_two, "head", 1)
    latent_low = grad_latent
    for bit in (1, 2):
        other = swap(latent_low, "head", bit)
        (latent_low,) = call(
            sum_body,
            (slots,),
            [
                by_slot(latent_low),
                (other, (None, rank, rows), functools.partial(lambda b, i, *_: (i ^ b, 0, 0), bit)),
            ],
            [out_by_slot((slots, rank, rows), f32 if bit == 1 else bf16)],
        )

    fixed, grad_normed = (), [None] * 4
    for slot in RING:
        extra = [whole(far)] if slot == 2 else []
        *fixed, grad_normed[slot] = call(
            project_back_body,
            (1,),
            [at_slot(a, slot) for a in (grad_pre, tail, arrived, grad_gate)]
            + [whole(w) for w in (query_weight, key_weight, value_weight, gate_weight)]
            + extra,
            [
                out_at_slot((slots, rows, all_cols), bf16, slot),
                out_whole((rows, width), f32 if slot == 0 else bf16),
            ],
            after={3: (feed_scattered, layer_two), 2: (latent_low,)}.get(slot, ()),
            into=fixed,
        )
        if slot == 3:
            far = swap(grad_normed[3], "head", 1)
    fixed = fixed[0]
    near = swap(grad_normed[1], "head", 1)
    far = swap(grad_normed[2], "head", 2)
    pre_pack = weight_grads([(normed, fixed, 0)], all_cols + 128, order, (grad_normed[0],), latent_low)
    layer_out = restored(0, layer_share, layer_one, bf16, (), (pre_pack,))
    (layer_out,) = restored(2, layer_two, layer_three, bf16, layer_out)
    token_share, small = call(
        first_back_body,
        (count,),
        [sequence(tokens, 0)]
        + tiles(grad_hidden_share, grad_normed[0], near, far)
        + [(latent_low, (None, rank, tile), lambda i, *_: (0, 0, i))]
        + [whole(decay_down), whole(mixer_norm.reshape(1, width))]
        + [whole(feed_norm_part), whole(small)],
        [
            ((rows, width), bf16, (tile, width), rowed),
            out_whole((2 * (width // KH) + small_rows, KH), f32),
        ],
        order=order,
        after=(pre_pack, layer_out),
    )
    one, two = swap(token_share, "head", 1), swap(token_share, "head", 2)
    token_grad = restored(0, token_share, one, f32)
    pre_scattered = scatter_sum(pre_pack, "seq", [(), (layer_out,), (token_share,)])

    small = total_sum(small, ("seq",))
    split = 2 * (width // KH)
    norms = total_sum(held(small[:split], tuple(token_grad)), ("head",))
    (token_grad,) = restored(2, two, swap(two, "head", 1), f32, token_grad, (norms,))
    norms = norms.reshape(2, width)
    group_gain_grad = small[split : split + 2].reshape(vals)
    decay_bias_grad = small[split + 2]
    decay_up_grad = small[split + 8 : split + 8 + rank]
    taps_grad = small[split + 8 + rank :].reshape(CONV, all_cols)

    return (
        layer_out,
        token_grad,
        norms[0],
        pre_scattered[:, :keys],
        pre_scattered[:, keys : 2 * keys],
        pre_scattered[:, 2 * keys : all_cols],
        side_scattered[:, vals:].astype(f32),
        pre_scattered[:, all_cols : all_cols + rank],
        decay_up_grad,
        decay_bias_grad,
        taps_grad[:, :keys],
        taps_grad[:, keys : 2 * keys],
        taps_grad[:, 2 * keys :],
        group_gain_grad,
        side_scattered[:, :vals].astype(f32).T,
        norms[1],
        feed_scattered[:, :hidden].astype(f32),
        feed_scattered[:, padded : padded + hidden].astype(f32),
        feed_scattered[:, 2 * padded : 2 * padded + hidden].astype(f32).T,
    )


def solution(mesh):
    placed = (
        P(None, "seq", None),
        P(None, "seq", None),
        P(),
        P(None, "head"),
        P(None, "head"),
        P(None, "head"),
        P(None, "head"),
        P(),
        P(None, "head"),
        P("head"),
        P(None, "head"),
        P(None, "head"),
        P(None, "head"),
        P("head"),
        P("head", None),
        P(),
        P(None, "head"),
        P(None, "head"),
        P("head", None),
    )
    return jax.shard_map(
        shards,
        mesh=mesh,
        in_specs=placed,
        out_specs=(
            P(None, "seq", None),
            P(None, "seq", None),
            P(),
            P("seq", "head"),
            P("seq", "head"),
            P("seq", "head"),
            P("seq", "head"),
            P("seq", None),
            P(None, "head"),
            P("head"),
            P(None, "head"),
            P(None, "head"),
            P(None, "head"),
            P("head"),
            P("head", "seq"),
            P(),
            P("seq", "head"),
            P("seq", "head"),
            P("head", "seq"),
        ),
        check_vma=False,
    )
```

```python
import functools

import functools

import jax
import jax.numpy as jnp
from jax import lax
from jax.experimental import pallas as pl
from jax.experimental.pallas import tpu as pltpu
from jax.sharding import PartitionSpec as P

KH = 128
VH = 256
STRETCH = 64
CONV = 4
SCALE = KH**-0.5
PAD = 8

epsilon = 1e-06
highest = lax.Precision.HIGHEST
f32 = jnp.float32
bf16 = jnp.bfloat16
VMEM = 50 * 1024 * 1024


def dot(a, b, dims=((1,), (0,)), precision=None):
    return lax.dot_general(a, b, (dims, ((), ())), precision=precision, preferred_element_type=f32)


NT = ((1,), (1,))
TN = ((0,), (0,))


def split_dot(left, values, dims=((1,), (0,))):
    high = values.astype(bf16)
    low = (values - high.astype(f32)).astype(bf16)
    return dot(left, high, dims) + dot(left, low, dims)


def two_pieces(values):
    high = values.astype(bf16)
    return high, (values - high.astype(f32)).astype(bf16)


def lower(span, strict=False):
    row = lax.broadcasted_iota(jnp.int32, (span, span), 0)
    col = lax.broadcasted_iota(jnp.int32, (span, span), 1)
    return (row > col) if strict else (row >= col)


def as_bf(mask):
    return jnp.where(mask, 1.0, 0.0).astype(bf16)


def call(body, grid, ins, outs, scratch=(), order=None, after=(), into=()):
    lead = [] if order is None else [order]
    arrays = lead + [entry[0] for entry in ins] + list(after) + list(into)
    in_specs = [
        pl.BlockSpec(memory_space=pltpu.SMEM) if entry[1] is None else pl.BlockSpec(entry[1], entry[2])
        for entry in ins
    ]
    in_specs += [pl.BlockSpec(memory_space=pl.ANY)] * (len(after) + len(into))
    first, skip = len(lead) + len(ins), len(after) + len(into)

    def run(*refs):
        body(*refs[len(lead) : first], *refs[first + skip :])

    return pl.pallas_call(
        run,
        out_shape=[jax.ShapeDtypeStruct(entry[0], entry[1]) for entry in outs],
        grid_spec=pltpu.PrefetchScalarGridSpec(
            num_scalar_prefetch=len(lead),
            grid=grid,
            in_specs=in_specs,
            out_specs=[pl.BlockSpec(entry[2], entry[3]) for entry in outs],
            scratch_shapes=list(scratch),
        ),
        input_output_aliases={first + len(after) + k: k for k in range(len(into))},
        compiler_params=pltpu.CompilerParams(vmem_limit_bytes=VMEM),
        cost_estimate=pl.CostEstimate(flops=1, bytes_accessed=1, transcendentals=0),
    )(*arrays)


def held(array, after):
    def body(*refs):
        pass

    return pl.pallas_call(
        body,
        out_shape=jax.ShapeDtypeStruct(array.shape, array.dtype),
        in_specs=[pl.BlockSpec(memory_space=pl.ANY)] * (1 + len(after)),
        out_specs=pl.BlockSpec(memory_space=pl.ANY),
        input_output_aliases={0: 0},
        cost_estimate=pl.CostEstimate(flops=1, bytes_accessed=1, transcendentals=0),
    )(array, *after)


def whole(array):
    zeros = (0,) * array.ndim
    return (array, array.shape, lambda *_: zeros)


def by_slot(array, base=0):
    rest = (0,) * (array.ndim - 1)
    return (array, (None,) + array.shape[1:], lambda i, *_: (i + base,) + rest)


def at_slot(array, slot):
    rest = (0,) * (array.ndim - 1)
    return (array, (None,) + array.shape[1:], lambda *_: (slot,) + rest)


def out_by_slot(shape, dtype, base=0):
    rest = (0,) * (len(shape) - 1)
    return (shape, dtype, (None,) + shape[1:], lambda i, *_: (i + base,) + rest)


def out_at_slot(shape, dtype, slot):
    rest = (0,) * (len(shape) - 1)
    return (shape, dtype, (None,) + shape[1:], lambda *_: (slot,) + rest)


def out_whole(shape, dtype):
    zeros = (0,) * len(shape)
    return (shape, dtype, shape, lambda *_: zeros)


def project_body(tokens, gain, w_query, w_key, w_value, normed, pre):
    values = tokens[...].astype(f32)
    scaled = values * lax.rsqrt(jnp.mean(values * values, axis=-1, keepdims=True) + epsilon)
    low = (scaled * gain[...]).astype(bf16)
    normed[...] = low
    keys, vals = w_query.shape[1], w_value.shape[1]
    pre[:, :keys] = dot(low, w_query[...]).astype(bf16)
    pre[:, keys : 2 * keys] = dot(low, w_key[...]).astype(bf16)
    pre[:, 2 * keys :] = dot(low, w_value[...]).astype(bf16)


def gate_body(normed, w_gate, w_down, gate_pre, latent):
    low = normed[...]
    gate_pre[...] = dot(low, w_gate[...])
    latent[...] = dot(low, w_down[...])


def conv_sum(scratch, taps, rows):
    summed = taps[0:1, :] * scratch[pl.ds(PAD - CONV + 1, rows), :]
    for offset in range(1, CONV):
        summed = summed + taps[offset : offset + 1, :] * scratch[
            pl.ds(PAD - CONV + 1 + offset, rows), :
        ]
    return summed


def decay_logits(latent, up, bias):
    return dot(latent[...], up[...], precision=highest) + bias[...]


def conv_body(
    pre, halo, taps, latent, up, bias,
    queries, key_vecs, val_vecs, inner_sum, starts, states, state_out, edges, message, ext,
):
    rows = pre.shape[0]
    ext[0:PAD, :] = halo[...].astype(f32)
    ext[PAD : PAD + rows, :] = pre[...].astype(f32)
    summed = conv_sum(ext, taps[...], rows)
    active = (summed * jax.nn.sigmoid(summed)).astype(bf16)
    queries[...] = active[:, :KH]
    key_vecs[...] = active[:, KH : 2 * KH]
    val_vecs[...] = active[:, 2 * KH :]
    logits = decay_logits(latent, up, bias)
    logdec = (jnp.minimum(logits, 0.0) - jnp.log1p(jnp.exp(-jnp.abs(logits)))) * (1.0 / 16.0)
    tril = jnp.where(lower(STRETCH), 1.0, 0.0)
    state = jnp.zeros((VH, KH), f32)
    before = jnp.zeros((1, KH), f32)
    for block in range(rows // STRETCH):
        at = slice(block * STRETCH, (block + 1) * STRETCH)
        total = dot(tril, logdec[at], precision=highest)
        inner_sum[at, :] = total
        last = total[STRETCH - 1 : STRETCH]
        starts[block : block + 1, :] = before
        states[block] = state
        carried = (active[at, KH : 2 * KH].astype(f32) * jnp.exp(last - total)).astype(bf16)
        state = state * jnp.exp(last) + dot(active[at, 2 * KH :], carried, TN)
        before = before + last
    state_out[...] = state
    decay = jnp.exp(before)
    edges[...] = jnp.where(first_row((8, KH)), decay, 1.0)
    pack_state(state, decay, message)


def first_row(shape, row=0):
    return lax.broadcasted_iota(jnp.int32, shape, 0) == row


def guess(column, line):
    one = jnp.where(first_row((16, column.shape[1])), column, 0.0).astype(bf16)
    two = jnp.where(first_row((16, line.shape[1])), line, 0.0).astype(bf16)
    return dot(one, two, TN)


def pack_state(state, decay, message):
    line = jnp.mean(state, axis=0, keepdims=True).astype(bf16).astype(f32)
    size = jnp.maximum(jnp.sum(line * line, axis=1, keepdims=True), 1e-30)
    lines = jnp.broadcast_to(line, (16, KH)).astype(bf16)
    column = dot(lines, state.astype(bf16), NT)[0:1] / size
    column = column.astype(bf16).astype(f32)
    message[0:VH, :] = (state - guess(column, line)).astype(bf16)
    high, low = two_pieces(decay)
    edge = jnp.zeros((16, KH), f32)
    for row, value in enumerate(
        (high.astype(f32), low.astype(f32), line, column[:, :KH], column[:, KH:])
    ):
        edge = jnp.where(first_row((16, KH), row), value, edge)
    message[VH:, :] = edge.astype(bf16)


def unpack_state(message):
    edge = message[VH:, :].astype(f32)
    column = jnp.concatenate([edge[3:4], edge[4:5]], axis=1)
    return message[0:VH, :].astype(f32) + guess(column, edge[2:3]), edge[0:1] + edge[1:2]


def is_later(place, level):
    return lax.rem(lax.div(place[0], 1 << level), 2) == 1


def combine_body(level, place, state, edges, result, other, *outs):
    theirs, their_decay = unpack_state(other)
    is_upper = is_later(place, level)
    own_decay, passed = edges[0:1, :], edges[1:2, :]
    new_result, new_edges = outs[0], outs[1]
    new_result[...] = result[...] + jnp.where(is_upper, passed * theirs, 0.0)
    low_decay = jnp.where(is_upper, their_decay, own_decay)
    high_decay = jnp.where(is_upper, own_decay, their_decay)
    both = low_decay * high_decay
    after = jnp.where(is_upper, passed * their_decay, passed)
    edge = jnp.zeros((8, KH), f32)
    for row, value in enumerate((both, after, their_decay, own_decay)):
        edge = jnp.where(first_row((8, KH), row), value, edge)
    new_edges[...] = edge
    if len(outs) > 2:
        own = state[...]
        joined = high_decay * jnp.where(is_upper, theirs, own) + jnp.where(is_upper, own, theirs)
        outs[2][...] = joined
        pack_state(joined, both, outs[3])


def halves(total):
    middle = total[STRETCH // 2 - 1 : STRETCH // 2]
    return jnp.exp(total - middle), jnp.exp(middle - total)


def close_scores(mask, ahead, behind):
    total = dot(ahead[0], behind[0], NT) + (
        dot(ahead[0], behind[1], NT) + dot(ahead[1], behind[0], NT)
    )
    return jnp.where(mask, total, 0.0)


def local_body(queries, key_vecs, val_vecs, inner_sum, states, attended):
    mask = lower(STRETCH)
    for block in range(queries.shape[0] // STRETCH):
        at = slice(block * STRETCH, (block + 1) * STRETCH)
        total = inner_sum[at, :]
        query = queries[at, :].astype(f32) * SCALE
        up, down = halves(total)
        scores, score_rest = two_pieces(
            close_scores(
                mask, two_pieces(query * up), two_pieces(key_vecs[at, :].astype(f32) * down)
            )
        )
        entering, rest = two_pieces(query * jnp.exp(total))
        high, low = two_pieces(states[block])
        attended[at, :] = (
            dot(scores, val_vecs[at, :])
            + dot(score_rest, val_vecs[at, :])
            + dot(entering, high, NT)
            + dot(entering, low, NT)
            + dot(rest, high, NT)
        )


def device_sum(inner_sum, starts):
    rows = inner_sum.shape[0]
    return jnp.concatenate(
        [
            inner_sum[block * STRETCH : (block + 1) * STRETCH, :] + starts[block : block + 1, :]
            for block in range(rows // STRETCH)
        ],
        axis=0,
    )


def mix_body(
    local, queries, inner_sum, starts, incoming, gate_pre, gain, w_out, *rest_refs
):
    attended, gated, mixed = rest_refs[-3:]
    total = device_sum(inner_sum, starts)
    entering, rest = two_pieces(queries[...].astype(f32) * SCALE * jnp.exp(total))
    high, low = two_pieces(incoming[...])
    values = local[...] + dot(entering, high, NT) + dot(entering, low, NT) + dot(rest, high, NT)
    attended[...] = values
    scaled = values * lax.rsqrt(jnp.mean(values * values, axis=-1, keepdims=True) + epsilon)
    gate = gate_pre[...]
    low = (scaled * gain[...] * (gate * jax.nn.sigmoid(gate))).astype(bf16)
    gated[...] = low
    summed = dot(low, w_out[...])
    if len(rest_refs) > 3:
        summed = summed + rest_refs[0][...].astype(f32)
    mixed[...] = summed.astype(mixed.dtype)


def restore_body(one, two, out):
    @pl.when(pl.program_id(0) == 0)
    def _():
        out[...] = one[...].astype(out.dtype)

    @pl.when(pl.program_id(0) == 1)
    def _():
        out[...] = two[...].astype(out.dtype)


def share_body(tokens, parts, near, far, gain, hidden, second):
    values = (
        tokens[...].astype(f32) + parts[...] + near[...].astype(f32) + far[...].astype(f32)
    )
    hidden[...] = values
    scaled = values * lax.rsqrt(jnp.mean(values * values, axis=-1, keepdims=True) + epsilon)
    second[...] = (scaled * gain[...]).astype(bf16)


def add_gain(out, first, values):
    @pl.when(pl.program_id(0) == 0)
    def _():
        out[first : first + values.shape[1] // KH, :] = jnp.zeros((values.shape[1] // KH, KH), f32)

    part = jnp.sum(values, axis=0, keepdims=True)
    for piece in range(values.shape[1] // KH):
        out[first + piece : first + piece + 1, :] += part[:, piece * KH : (piece + 1) * KH]


def share_back_body(hidden, cotangent, parts, near, far, gain, grad_hidden, low, gain_part):
    grad = parts[...] + near[...].astype(f32) + far[...].astype(f32)
    values = hidden[...]
    inverse = lax.rsqrt(jnp.mean(values * values, axis=-1, keepdims=True) + epsilon)
    scaled = values * inverse
    add_gain(gain_part, 0, grad * scaled)
    inner = grad * gain[...]
    inner = inverse * (inner - scaled * jnp.mean(inner * scaled, axis=-1, keepdims=True))
    total = cotangent[...].astype(f32) + inner
    grad_hidden[...] = total
    low[...] = total.astype(bf16)


def sum_body(one, two, out):
    out[...] = (one[...] + two[...]).astype(out.dtype)


def join_body(one, two, out):
    out[...] = (one[...] + two[...].astype(f32)).astype(out.dtype)


def layer_body(hidden, parts, near, far, out):
    total = hidden[...] + parts[...] + near[...].astype(f32) + far[...].astype(f32)
    out[...] = total.astype(out.dtype)


def feed_body(
    normed, cotangent, w_gate, w_up, w_down, inner, grad_gate, grad_up, grad_normed, feed_out
):
    low = normed[...]
    gate = dot(low, w_gate[...])
    up = dot(low, w_up[...])
    grad = dot(cotangent[...], w_down[...], NT)
    soft = jax.nn.sigmoid(gate)
    silu = gate * soft
    product = (silu * up).astype(bf16)
    inner[...] = product
    gate_low = (grad * up * (soft * (1.0 + gate * (1.0 - soft)))).astype(bf16)
    up_low = (grad * silu).astype(bf16)
    grad_gate[...] = gate_low
    grad_up[...] = up_low
    feed_out[...] = dot(product, w_down[...]).astype(feed_out.dtype)
    summed = dot(gate_low, w_gate[...], NT) + dot(up_low, w_up[...], NT)
    grad_normed[...] = summed.astype(grad_normed.dtype)


def gate_back_body(
    grad_hidden, w_out, attended, gate_pre, gain, queries, inner_sum, starts,
    grad_attended, grad_gate, state, message, gain_part,
):
    grad = dot(grad_hidden[...], w_out[...], NT)
    values = attended[...]
    inverse = lax.rsqrt(jnp.mean(values * values, axis=-1, keepdims=True) + epsilon)
    scaled = values * inverse
    gate = gate_pre[...]
    soft = jax.nn.sigmoid(gate)
    grad_gate[...] = (
        grad * scaled * gain[...] * (soft * (1.0 + gate * (1.0 - soft)))
    ).astype(bf16)
    grad = grad * (gate * soft)
    gain_part[...] = jnp.broadcast_to(jnp.sum(grad * scaled, axis=0, keepdims=True), gain_part.shape)
    grad = grad * gain[...]
    grad = inverse * (grad - scaled * jnp.mean(grad * scaled, axis=-1, keepdims=True))
    grad_attended[...] = grad
    high, low = two_pieces(grad)
    total = device_sum(inner_sum, starts)
    entering = (queries[...].astype(f32) * SCALE * jnp.exp(total)).astype(bf16)
    summed = dot(high, entering, TN) + dot(low, entering, TN)
    state[...] = summed
    message[...] = summed.astype(message.dtype)


def local_back_body(
    queries, key_vecs, val_vecs, inner_sum, starts, states, incoming, grad_attended,
    grad_queries, grad_keys, grad_vals, grad_logdec,
):
    mask = lower(STRETCH)
    row = lax.broadcasted_iota(jnp.int32, (STRETCH, 2 * STRETCH), 0)
    col = lax.broadcasted_iota(jnp.int32, (STRETCH, 2 * STRETCH), 1)
    later = jnp.where(col >= row, 1.0, 0.0)
    earlier = jnp.where(col - STRETCH < row, 1.0, 0.0)
    sums = jnp.where(col < STRETCH, later, earlier).astype(bf16)
    running = jnp.zeros((VH, KH), f32)
    entered = incoming[...]
    for block in reversed(range(queries.shape[0] // STRETCH)):
        at = slice(block * STRETCH, (block + 1) * STRETCH)
        total = inner_sum[at, :]
        last = total[STRETCH - 1 : STRETCH]
        query = queries[at, :].astype(f32) * SCALE
        key = key_vecs[at, :].astype(f32)
        val = val_vecs[at, :]
        grad, grad_rest = two_pieces(grad_attended[at, :])
        up, down = halves(total)
        whole_up = jnp.exp(total)
        rest = jnp.exp(last - total)
        ahead, ahead_rest = two_pieces(query * up)
        behind, behind_rest = two_pieces(key * down)
        entering = (query * whole_up).astype(bf16)
        carried = (key * rest).astype(bf16)
        current = states[block] + entered * jnp.exp(starts[block : block + 1, :])
        scores = close_scores(mask, (ahead, ahead_rest), (behind, behind_rest)).astype(bf16)
        grad_scores = jnp.where(mask, dot(grad, val, NT) + dot(grad_rest, val, NT), 0.0).astype(bf16)
        running_low, running_rest = two_pieces(running)
        current_low, current_rest = two_pieces(current)
        grad_ahead = dot(grad_scores, behind)
        grad_behind = dot(grad_scores, ahead, TN)
        grad_entering = (
            dot(grad, current_low) + dot(grad, current_rest) + dot(grad_rest, current_low)
        )
        grad_carried = dot(val, running_low) + dot(val, running_rest)
        grad_vals[at, :] = dot(scores, grad, TN) + dot(carried, running_low, NT)
        grad_queries[at, :] = (grad_ahead * up + grad_entering * whole_up) * SCALE
        grad_keys[at, :] = grad_behind * down + grad_carried * rest
        inside = (
            ahead.astype(f32) * grad_ahead
            - behind.astype(f32) * grad_behind
            + entering.astype(f32) * grad_entering
        )
        stacked = jnp.concatenate([inside, carried.astype(f32) * grad_carried], axis=0)
        through = jnp.sum(current * running, axis=0, keepdims=True) * jnp.exp(last)
        grad_logdec[at, :] = split_dot(sums, stacked) + through
        running = running * jnp.exp(last) + dot(grad, entering, TN) + dot(grad_rest, entering, TN)


def conv_back_body(
    grad_queries, grad_keys, grad_vals, grad_logdec, key_vecs, val_vecs, inner_sum, starts,
    incoming, outgoing, pre, halo, taps, latent, up, bias,
    gain_zero, gain_one, gain_two, gain_three,
    grad_pre, tail, head, grad_latent, small, ext, back,
):
    rows = pre.shape[0]
    keys = grad_queries.shape[1]
    ext[0:PAD, :] = halo[...].astype(f32)
    ext[PAD : PAD + rows, :] = pre[...].astype(f32)
    summed = conv_sum(ext, taps[...], rows)
    soft = jax.nn.sigmoid(summed)
    slope = soft * (1.0 + summed * (1.0 - soft))
    total = device_sum(inner_sum, starts)
    final = total[rows - 1 : rows]
    rest = jnp.exp(final - total)
    leaving, leaving_rest = two_pieces(outgoing[...])
    carried = (key_vecs[...].astype(f32) * rest).astype(bf16)
    grad_carried = dot(val_vecs[...], leaving) + dot(val_vecs[...], leaving_rest)
    back[0:PAD, :] = jnp.zeros((PAD, back.shape[1]), f32)
    back[PAD + rows :, :] = jnp.zeros((PAD, back.shape[1]), f32)
    back[PAD : PAD + rows, 0:keys] = grad_queries[...] * slope[:, 0:keys]
    back[PAD : PAD + rows, keys : 2 * keys] = (grad_keys[...] + grad_carried * rest) * slope[
        :, keys : 2 * keys
    ]
    back[PAD : PAD + rows, 2 * keys :] = (grad_vals[...] + dot(carried, leaving, NT)) * slope[
        :, 2 * keys :
    ]
    pairs = carried.astype(f32) * grad_carried
    strict = as_bf(lower(STRETCH, True))
    through = jnp.sum(incoming[...] * outgoing[...], axis=0, keepdims=True) * jnp.exp(final)
    logits = decay_logits(latent, up, bias)
    fade = jax.nn.sigmoid(-logits) * (1.0 / 16.0)
    pieces = []
    for block in range(rows // STRETCH):
        at = slice(block * STRETCH, (block + 1) * STRETCH)
        pieces.append(grad_logdec[at, :] + split_dot(strict, pairs[at]) + through)
        through = through + jnp.sum(pairs[at], axis=0, keepdims=True)
    grad_logits = jnp.concatenate(pieces, axis=0) * fade
    gains = gain_zero[0:1, :] + gain_one[0:1, :] + gain_two[0:1, :] + gain_three[0:1, :]

    @pl.when(pl.program_id(0) == 0)
    def _():
        small[...] = jnp.zeros(small.shape, f32)
        small[0:1, :] = gains[:, :KH]
        small[1:2, :] = gains[:, KH:]

    small[2:3, :] += jnp.sum(grad_logits, axis=0, keepdims=True)
    rank = latent.shape[1]
    small[8 : 8 + rank, :] += dot(latent[...], grad_logits, TN, highest)
    grad_latent[...] = dot(up[...], grad_logits, NT, highest)
    kernel = taps[...]
    grad = kernel[0:1, :] * back[pl.ds(CONV - 1, PAD + rows), :]
    for offset in range(1, CONV):
        grad = grad + kernel[offset : offset + 1, :] * back[
            pl.ds(CONV - 1 - offset, PAD + rows), :
        ]
    head[...] = grad[0:PAD]
    tail[...] = grad[rows:]
    grad_pre[...] = grad[PAD:].astype(bf16)
    inner = back[PAD : PAD + rows, :]
    for offset in range(CONV):
        part = jnp.sum(
            inner * ext[pl.ds(PAD - CONV + 1 + offset, rows), :], axis=0, keepdims=True
        )
        for piece in range(part.shape[1] // KH):
            row = 8 + rank + offset * (part.shape[1] // KH) + piece
            small[row : row + 1, :] += part[:, piece * KH : (piece + 1) * KH]


def project_back_body(
    grad_pre, tail, arrived, grad_gate, w_query, w_key, w_value, w_gate, *rest_refs
):
    fixed, grad_normed = rest_refs[-2:]
    rows = grad_pre.shape[0]
    keys = w_query.shape[1]
    fixed[0 : rows - 16, :] = grad_pre[0 : rows - 16, :]
    ending = jnp.concatenate(
        [grad_pre[rows - 16 : rows, :].astype(f32)[0 : 16 - PAD], tail[...] + arrived[...]], axis=0
    )
    fixed[rows - 16 : rows, :] = ending.astype(bf16)
    low = fixed[...]
    summed = dot(low[:, 0:keys], w_query[...], NT) + dot(low[:, keys : 2 * keys], w_key[...], NT)
    summed = summed + dot(low[:, 2 * keys :], w_value[...], NT)
    summed = summed + dot(grad_gate[...], w_gate[...], NT)
    if len(rest_refs) > 2:
        summed = summed + rest_refs[0][...].astype(f32)
    grad_normed[...] = summed.astype(grad_normed.dtype)


def first_back_body(
    tokens, grad_hidden, parts, near, far, latent, w_down, gain, others, small, token_grad, sums
):
    grad = parts[...] + near[...].astype(f32) + far[...].astype(f32)
    grad = grad + dot(latent[...], w_down[...], ((0,), (1,)))
    values = tokens[...].astype(f32)
    inverse = lax.rsqrt(jnp.mean(values * values, axis=-1, keepdims=True) + epsilon)
    scaled = values * inverse
    count = others.shape[0]
    add_gain(sums, 0, grad * scaled)
    sums[count : 2 * count, :] = others[...]
    sums[2 * count :, :] = small[...]
    inner = grad * gain[...]
    inner = inverse * (inner - scaled * jnp.mean(inner * scaled, axis=-1, keepdims=True))
    token_grad[...] = (grad_hidden[...] + inner).astype(bf16)


def weight_grads(jobs, width, order=None, after=(), latent=None, blocks=4):
    arrays, plan, ins = [], [], []
    depth = width_of = None
    for left, right, first in jobs:
        entry = []
        for side, group in ((0, left), (1, right)):
            places = []
            if side == 0 and not isinstance(group, list) and order is not None and latent is None:
                group = [(group, slot) for slot in range(group.shape[0])]
            for item in group if isinstance(group, list) else [group]:
                array, slot = item if isinstance(item, tuple) else (item, None)
                known = [k for k, a in enumerate(arrays) if a[0] is array and a[1:] == (side, slot)]
                if not known:
                    arrays.append((array, side, slot))
                    known = [len(arrays) - 1]
                places.append(known[0])
            entry.append(places)
        plan.append((entry[0], entry[1], first))
    depth = arrays[0][0].shape[-1]
    block = depth // blocks
    for array, side, slot in arrays:
        if side == 1:
            ins.append(whole(array))
        elif slot is not None:
            ins.append(
                (
                    array,
                    (None, array.shape[1], block),
                    functools.partial(lambda k, i, ref: (ref[k], 0, i), slot),
                )
            )
        elif array.ndim == 2:
            ins.append((array, (array.shape[0], block), lambda i, *_: (0, i)))
        else:
            ins.append((array, array.shape[:2] + (block,), lambda i, *_: (0, 0, i)))
    if latent is not None:
        ins.append((order, None, None))
        ins.append(whole(latent))

    def body(*refs):
        out = refs[len(ins)]
        covered = 0
        for lefts, rights, first in plan:
            total = None
            pairs = []
            for left, right in zip(lefts, rights):
                a, b = refs[left], refs[right]
                if len(a.shape) == 2:
                    pairs.append((a, b))
                else:
                    pairs += [(a.at[k], b.at[k]) for k in range(a.shape[0])]
            for one, two in pairs:
                term = dot(one[...], two[...], TN)
                total = term if total is None else total + term
            if first > covered:
                out[:, covered:first] = jnp.zeros((block, first - covered), bf16)
            out[:, first : first + total.shape[1]] = total.astype(bf16)
            covered = first + total.shape[1]
        if covered < width:
            out[:, covered:] = jnp.zeros((block, width - covered), bf16)
        if latent is not None:
            place, factor, parts = refs[len(ins) - 2], refs[len(ins) - 1], refs[len(ins) + 1]
            one = refs[plan[0][0][0]]
            for slot in range(factor.shape[0]):
                parts[place[slot]] = dot(one[slot], factor[slot], ((0,), (1,)))
            total = parts[0]
            for sequence in range(1, factor.shape[0]):
                total = total + parts[sequence]
            out[:, covered : covered + total.shape[1]] = total.astype(bf16)

    return call(
        body,
        (blocks,),
        ins,
        [((depth, width), bf16, (block, width), lambda i, *_: (i, 0))],
        [] if latent is None else [pltpu.VMEM((latent.shape[0], block, latent.shape[1]), f32)],
        order=order if latent is None else None,
        after=after,
    )[0]


def bits_of(axis):
    count = lax.axis_size(axis)
    return [1 << k for k in range(count.bit_length() - 1)]


def swap(value, axis, bit):
    count = lax.axis_size(axis)
    return lax.ppermute(value, axis, [(source, source ^ bit) for source in range(count)])


def passed_along(value, axis, steps):
    count = lax.axis_size(axis)
    first, last = (max(0, -steps), min(count, count - steps))
    return lax.ppermute(value, axis, [(source, source + steps) for source in range(first, last)])


def combine_back_body(level, place, state, edges, behind, result, other, *outs):
    theirs = other[...].astype(f32)
    is_upper = is_later(place, level)
    their_decay, own_decay = edges[2:3, :], edges[3:4, :]
    passed = behind[0:1, :]
    outs[0][...] = result[...] + jnp.where(is_upper, 0.0, passed * theirs)
    outs[1][...] = jnp.broadcast_to(jnp.where(is_upper, passed, passed * their_decay), behind.shape)
    if len(outs) > 2:
        own = state[...]
        low_decay = jnp.where(is_upper, their_decay, own_decay)
        joined = jnp.where(is_upper, theirs, own) + low_decay * jnp.where(is_upper, own, theirs)
        outs[2][...] = joined
        outs[3][...] = joined.astype(bf16)


def entering_states(place, state, edges, message, fillers):
    slots = state.shape[0]
    result = jnp.zeros_like(state)
    kept = []
    bits = bits_of("seq")
    for level, bit in enumerate(bits):
        other = swap(message, "seq", bit)
        beside = fillers[level](message) if level < len(fillers) else ()
        last = level + 1 == len(bits)
        outs = [out_by_slot((slots, VH, KH), f32), out_by_slot((slots, 8, KH), f32)]
        if not last:
            outs += [out_by_slot((slots, VH, KH), f32), out_by_slot((slots, VH + 16, KH), bf16)]
        given = call(
            functools.partial(combine_body, level),
            (slots,),
            [place] + [by_slot(a) for a in (state, edges, result, other)],
            outs,
            after=beside,
        )
        result, edges = given[0], given[1]
        kept.append(edges)
        if not last:
            state, message = given[2], given[3]
    return result, kept


def leaving_states(place, state, message, kept, fillers):
    slots = state.shape[0]
    result = jnp.zeros_like(state)
    behind = jnp.ones((slots, 8, KH), f32)
    bits = bits_of("seq")
    for level, bit in enumerate(bits):
        other = swap(message, "seq", bit)
        beside = fillers[level](message) if level < len(fillers) else ()
        last = level + 1 == len(bits)
        outs = [out_by_slot((slots, VH, KH), f32), out_by_slot((slots, 8, KH), f32)]
        if not last:
            outs += [out_by_slot((slots, VH, KH), f32), out_by_slot((slots, VH, KH), bf16)]
        given = call(
            functools.partial(combine_back_body, level),
            (slots,),
            [place] + [by_slot(a) for a in (state, kept[level], behind, result, other)],
            outs,
            after=beside,
        )
        result, behind = given[0], given[1]
        if not last:
            state, message = given[2], given[3]
    return result


def total_sum(value, axes):
    for axis in axes:
        for bit in bits_of(axis):
            value = value + swap(value, axis, bit)
    return value


def scatter_sum(value, axis, after):
    place = lax.axis_index(axis).astype(jnp.uint32)
    parts = lax.axis_size(axis)
    columns = value.shape[1]
    block = value.shape[0] // parts
    current = value
    for level, bit in enumerate(bits_of(axis)):
        if level < len(after) and after[level]:
            current = held(current, after[level])
        mine = (place // bit) % 2
        pairs = current.reshape(parts // (2 * bit), 2, block, columns)
        zero = jnp.uint32(0)
        shape = (parts // (2 * bit), 1, block, columns)
        kept = lax.dynamic_slice(pairs, (zero, mine, zero, zero), shape)
        sent = lax.dynamic_slice(pairs, (zero, 1 - mine, zero, zero), shape)
        got = swap(sent.astype(bf16), axis, bit)
        current = kept.astype(f32) + got.astype(f32)
        if 2 * bit < parts:
            current = current.astype(bf16)
    return current.reshape(block, columns)


def gather_slots(own):
    one = swap(own, "head", 1)
    two = swap(own, "head", 2)
    three = swap(two, "head", 1)
    return [own, one, two, three]


RING = (3, 1, 2, 0)


def shards(
    tokens,
    cotangent,
    mixer_norm,
    query_weight,
    key_weight,
    value_weight,
    gate_weight,
    decay_down,
    decay_up,
    decay_bias,
    query_conv,
    key_conv,
    value_conv,
    group_gain,
    output_weight,
    feed_norm,
    feed_gate,
    feed_up,
    feed_down,
):
    slots, rows, width = tokens.shape
    keys = query_weight.shape[1]
    vals = value_weight.shape[1]
    hidden = feed_gate.shape[1]
    rank = decay_down.shape[1]
    all_cols = 2 * keys + vals
    blocks = rows // STRETCH
    assert slots == lax.axis_size("head") == 4 and keys == KH and vals == VH
    me = lax.axis_index("head")
    place = lax.axis_index("seq").astype(jnp.int32).reshape(1)
    place = (place, None, None)
    order = jnp.bitwise_xor(jnp.arange(slots, dtype=jnp.int32), me.astype(jnp.int32))

    tile = min(256, rows)
    count = rows // tile
    rowed = lambda i, *_: (i, 0)

    def tiles(*arrays):
        return [(array, (tile, array.shape[1]), rowed) for array in arrays]

    def sequence(array, slot):
        return (array, (None, tile, width), lambda i, order_ref: (order_ref[slot], i, 0))

    def restored(base, one, two, dtype, into=(), after=()):
        return call(
            restore_body,
            (2, count),
            [
                (one, (tile, width), lambda s, i, *_: (jnp.where(s == 0, i, count - 1), 0)),
                (two, (tile, width), lambda s, i, *_: (jnp.where(s == 1, i, 0), 0)),
            ],
            [
                (
                    (slots, rows, width),
                    dtype,
                    (None, tile, width),
                    lambda s, i, order_ref: (order_ref[base + s], i, 0),
                )
            ],
            order=order,
            after=after,
            into=into,
        )

    taps = jnp.concatenate([query_conv, key_conv, value_conv], axis=-1)
    gain_row = group_gain.reshape(1, vals)
    bias_row = decay_bias.reshape(1, keys)

    normed, pre = call(
        project_body,
        (slots,),
        [
            (tokens, (None, rows, width), lambda i, order_ref: (order_ref[i], 0, 0)),
            whole(mixer_norm.reshape(1, width)),
            whole(query_weight),
            whole(key_weight),
            whole(value_weight),
        ],
        [
            out_by_slot((slots, rows, width), bf16),
            out_by_slot((slots, rows, all_cols), bf16),
        ],
        order=order,
    )
    halo = passed_along(pre[:, rows - PAD :, :], "seq", 1)
    gate_pre, latent = call(
        gate_body,
        (slots,),
        [by_slot(normed), whole(gate_weight), whole(decay_down)],
        [
            out_by_slot((slots, rows, vals), f32),
            out_by_slot((slots, rows, rank), f32),
        ],
    )
    queries, key_vecs, val_vecs, inner_sum, starts, states, total, edges, message = call(
        conv_body,
        (slots,),
        [
            by_slot(pre),
            by_slot(halo),
            whole(taps),
            by_slot(latent),
            whole(decay_up),
            whole(bias_row),
        ],
        [
            out_by_slot((slots, rows, keys), bf16),
            out_by_slot((slots, rows, keys), bf16),
            out_by_slot((slots, rows, vals), bf16),
            out_by_slot((slots, rows, keys), f32),
            out_by_slot((slots, blocks, keys), f32),
            out_by_slot((slots, blocks, VH, KH), f32),
            out_by_slot((slots, VH, KH), f32),
            out_by_slot((slots, 8, KH), f32),
            out_by_slot((slots, VH + 16, KH), bf16),
        ],
        [pltpu.VMEM((PAD + rows, all_cols), f32)],
    )
    local = ()

    def local_part(base):
        def make(message):
            nonlocal local
            local = call(
                local_body,
                (2,),
                [by_slot(a, base) for a in (queries, key_vecs, val_vecs, inner_sum, states)],
                [out_by_slot((slots, rows, vals), f32, base)],
                after=(message,),
                into=local,
            )
            return tuple(local)

        return make

    incoming, kept = entering_states(
        place,
        total,
        edges,
        message,
        [local_part(0), local_part(2), lambda message: (feed_gate, feed_up)],
    )
    local = local[0]

    attended, gated, mixed = [None] * 4, [None] * 4, [None] * 4
    done = ()
    far = None
    for slot in RING:
        extra = [whole(far)] if slot == 2 else []
        attended[slot], gated[slot], mixed[slot] = call(
            mix_body,
            (1,),
            [at_slot(a, slot) for a in (local, queries, inner_sum, starts, incoming, gate_pre)]
            + [whole(gain_row), whole(output_weight)]
            + extra,
            [
                out_whole((rows, vals), f32),
                out_whole((rows, vals), bf16),
                out_whole((rows, width), f32 if slot == 0 else bf16),
            ],
            after=done,
        )
        done = (mixed[slot],)
        if slot == 3:
            far = swap(mixed[3], "head", 1)
    near = swap(mixed[1], "head", 1)
    far = swap(mixed[2], "head", 2)
    norm_row = feed_norm.reshape(1, width)
    hidden_share, second = call(
        share_body,
        (rows // tile,),
        [sequence(tokens, 0)] + tiles(mixed[0], near, far) + [whole(norm_row)],
        [((rows, width), f32, (tile, width), rowed), ((rows, width), bf16, (tile, width), rowed)],
        order=order,
    )
    one, two = swap(second, "head", 1), swap(second, "head", 2)
    second_all = [second, one, None, None]

    inner, grad_gates, grad_ups, grad_seconds, feed_outs = ([None] * 4 for _ in range(5))
    done = ()
    for slot in (0, 1, 2, 3):
        wide = bf16 if slot % 2 else f32
        if slot == 2:
            second_all[2] = held(two, done)
            second_all[3] = swap(second_all[2], "head", 1)
        inner[slot], grad_gates[slot], grad_ups[slot], grad_seconds[slot], feed_outs[slot] = call(
            feed_body,
            (rows // tile,),
            tiles(second_all[slot])
            + [sequence(cotangent, slot)]
            + [whole(feed_gate), whole(feed_up), whole(feed_down)],
            [
                ((rows, hidden), bf16, (tile, hidden), rowed),
                ((rows, hidden), bf16, (tile, hidden), rowed),
                ((rows, hidden), bf16, (tile, hidden), rowed),
                ((rows, width), wide, (tile, width), rowed),
                ((rows, width), wide, (tile, width), rowed),
            ],
            order=order,
            after=done,
        )
        done = (inner[slot],)
    near = swap(grad_seconds[1], "head", 1)
    far = swap(grad_seconds[3], "head", 1)
    (joined,) = call(
        join_body,
        (count,),
        tiles(grad_seconds[2], far),
        [((rows, width), bf16, (tile, width), rowed)],
    )
    far = swap(joined, "head", 2)
    padded = -(-hidden // 128) * 128
    feed_pack = weight_grads(
        [
            (second_all, grad_gates, 0),
            (second_all, grad_ups, padded),
            (cotangent, inner, 2 * padded),
        ],
        3 * padded,
        order,
        (joined,),
    )
    grad_hidden_share, grad_hidden_low, feed_norm_part = call(
        share_back_body,
        (rows // tile,),
        tiles(hidden_share)
        + [sequence(cotangent, 0)]
        + tiles(grad_seconds[0], near, far)
        + [whole(norm_row)],
        [
            ((rows, width), f32, (tile, width), rowed),
            ((rows, width), bf16, (tile, width), rowed),
            out_whole((width // KH, KH), f32),
        ],
        order=order,
        after=(feed_pack,),
    )
    feed_scattered = lax.psum_scatter(
        held(feed_pack, (grad_hidden_low,)), "seq", scatter_dimension=0, tiled=True
    )
    one, two = swap(grad_hidden_low, "head", 1), swap(grad_hidden_low, "head", 2)
    grad_low = [grad_hidden_low, one, None, None]

    stacks, gain_parts = (), [None] * 4
    for slot in (0, 1, 2, 3):
        if slot == 2:
            grad_low[2] = held(two, stacks[:1])
            grad_low[3] = swap(grad_low[2], "head", 1)
        *stacks, gain_parts[slot] = call(
            gate_back_body,
            (1,),
            [whole(grad_low[slot]), whole(output_weight), whole(attended[slot])]
            + [at_slot(gate_pre, slot), whole(gain_row)]
            + [at_slot(a, slot) for a in (queries, inner_sum, starts)],
            [
                out_at_slot((slots, rows, vals), f32, slot),
                out_at_slot((slots, rows, vals), bf16, slot),
                out_at_slot((slots, VH, KH), f32, slot),
                out_at_slot((slots, VH, KH), bf16, slot),
                out_whole((8, vals), f32),
            ],
            into=stacks,
        )
    grad_attended, grad_gate, back_state, back_message = stacks

    feed_far = swap(held(feed_outs[3], (back_message,)), "head", 1)
    feed_near = swap(feed_outs[1], "head", 1)

    def layer_sum(message):
        nonlocal feed_far
        (joined,) = call(
            join_body,
            (count,),
            tiles(feed_outs[2], feed_far),
            [((rows, width), bf16, (tile, width), rowed)],
        )
        feed_far = swap(joined, "head", 2)
        return (joined,)

    grad_local = ()

    def back_part(base):
        def make(message):
            nonlocal grad_local
            grad_local = call(
                local_back_body,
                (2,),
                [
                    by_slot(a, base)
                    for a in (
                        queries, key_vecs, val_vecs, inner_sum, starts, states, incoming, grad_attended,
                    )
                ],
                [
                    out_by_slot((slots, rows, keys), f32, base),
                    out_by_slot((slots, rows, keys), f32, base),
                    out_by_slot((slots, rows, vals), f32, base),
                    out_by_slot((slots, rows, keys), f32, base),
                ],
                after=(message,) + (layer_sum(message) if base == 0 else ()),
                into=grad_local,
            )
            return (grad_local[0],)

        return make

    def side_part(message):
        nonlocal side_pack
        side_pack = weight_grads(
            [(grad_low, gated, 0), (normed, grad_gate, vals)], 2 * vals, None, (message,)
        )
        return (side_pack,)

    side_pack = None
    outgoing = leaving_states(
        place, back_state, back_message, kept, [back_part(0), back_part(2), side_part]
    )
    side_scattered = lax.psum_scatter(
        held(side_pack, (outgoing,)), "seq", scatter_dimension=0, tiled=True
    )
    (layer_share,) = call(
        layer_body,
        (count,),
        tiles(hidden_share, feed_outs[0], feed_near, feed_far),
        [((rows, width), bf16, (tile, width), rowed)],
        after=(outgoing,),
    )
    layer_one, layer_two = swap(layer_share, "head", 1), swap(layer_share, "head", 2)
    small_rows = 8 + rank + CONV * all_cols // KH
    grad_pre, tail, head, grad_latent, small = call(
        conv_back_body,
        (slots,),
        [by_slot(a) for a in grad_local]
        + [by_slot(a) for a in (key_vecs, val_vecs, inner_sum, starts, incoming, outgoing)]
        + [by_slot(pre), by_slot(halo), whole(taps), by_slot(latent), whole(decay_up)]
        + [whole(bias_row)]
        + [whole(part) for part in gain_parts],
        [
            out_by_slot((slots, rows, all_cols), bf16),
            out_by_slot((slots, PAD, all_cols), f32),
            out_by_slot((slots, PAD, all_cols), f32),
            out_by_slot((slots, rank, rows), f32),
            out_whole((small_rows, KH), f32),
        ],
        [
            pltpu.VMEM((PAD + rows, all_cols), f32),
            pltpu.VMEM((2 * PAD + rows, all_cols), f32),
        ],
        after=(layer_share,),
    )
    arrived = passed_along(head, "seq", -1)
    layer_two = held(layer_two, (grad_pre,))
    layer_three = swap(layer_two, "head", 1)
    latent_low = grad_latent
    for bit in (1, 2):
        other = swap(latent_low, "head", bit)
        (latent_low,) = call(
            sum_body,
            (slots,),
            [
                by_slot(latent_low),
                (other, (None, rank, rows), functools.partial(lambda b, i, *_: (i ^ b, 0, 0), bit)),
            ],
            [out_by_slot((slots, rank, rows), f32 if bit == 1 else bf16)],
        )

    fixed, grad_normed = (), [None] * 4
    for slot in RING:
        extra = [whole(far)] if slot == 2 else []
        *fixed, grad_normed[slot] = call(
            project_back_body,
            (1,),
            [at_slot(a, slot) for a in (grad_pre, tail, arrived, grad_gate)]
            + [whole(w) for w in (query_weight, key_weight, value_weight, gate_weight)]
            + extra,
            [
                out_at_slot((slots, rows, all_cols), bf16, slot),
                out_whole((rows, width), f32 if slot == 0 else bf16),
            ],
            after={3: (feed_scattered, layer_two), 2: (latent_low,)}.get(slot, ()),
            into=fixed,
        )
        if slot == 3:
            far = swap(grad_normed[3], "head", 1)
    fixed = fixed[0]
    near = swap(grad_normed[1], "head", 1)
    far = swap(grad_normed[2], "head", 2)
    pre_pack = weight_grads([(normed, fixed, 0)], all_cols + 128, order, (grad_normed[0],), latent_low)
    layer_out = restored(0, layer_share, layer_one, bf16, (), (pre_pack,))
    (layer_out,) = restored(2, layer_two, layer_three, bf16, layer_out)
    token_share, small = call(
        first_back_body,
        (count,),
        [sequence(tokens, 0)]
        + tiles(grad_hidden_share, grad_normed[0], near, far)
        + [(latent_low, (None, rank, tile), lambda i, *_: (0, 0, i))]
        + [whole(decay_down), whole(mixer_norm.reshape(1, width))]
        + [whole(feed_norm_part), whole(small)],
        [
            ((rows, width), bf16, (tile, width), rowed),
            out_whole((2 * (width // KH) + small_rows, KH), f32),
        ],
        order=order,
        after=(pre_pack, layer_out),
    )
    one, two = swap(token_share, "head", 1), swap(token_share, "head", 2)
    token_grad = restored(0, token_share, one, f32)
    pre_scattered = scatter_sum(pre_pack, "seq", [(), (layer_out,), (token_share,)])

    small = total_sum(small, ("seq",))
    split = 2 * (width // KH)
    norms = total_sum(held(small[:split], tuple(token_grad)), ("head",))
    (token_grad,) = restored(2, two, swap(two, "head", 1), f32, token_grad, (norms,))
    norms = norms.reshape(2, width)
    group_gain_grad = small[split : split + 2].reshape(vals)
    decay_bias_grad = small[split + 2]
    decay_up_grad = small[split + 8 : split + 8 + rank]
    taps_grad = small[split + 8 + rank :].reshape(CONV, all_cols)

    return (
        layer_out,
        token_grad,
        norms[0],
        pre_scattered[:, :keys],
        pre_scattered[:, keys : 2 * keys],
        pre_scattered[:, 2 * keys : all_cols],
        side_scattered[:, vals:].astype(f32),
        pre_scattered[:, all_cols : all_cols + rank],
        decay_up_grad,
        decay_bias_grad,
        taps_grad[:, :keys],
        taps_grad[:, keys : 2 * keys],
        taps_grad[:, 2 * keys :],
        group_gain_grad,
        side_scattered[:, :vals].astype(f32).T,
        norms[1],
        feed_scattered[:, :hidden].astype(f32),
        feed_scattered[:, padded : padded + hidden].astype(f32),
        feed_scattered[:, 2 * padded : 2 * padded + hidden].astype(f32).T,
    )


def solution(mesh):
    placed = (
        P(None, "seq", None),
        P(None, "seq", None),
        P(),
        P(None, "head"),
        P(None, "head"),
        P(None, "head"),
        P(None, "head"),
        P(),
        P(None, "head"),
        P("head"),
        P(None, "head"),
        P(None, "head"),
        P(None, "head"),
        P("head"),
        P("head", None),
        P(),
        P(None, "head"),
        P(None, "head"),
        P("head", None),
    )
    return jax.shard_map(
        shards,
        mesh=mesh,
        in_specs=placed,
        out_specs=(
            P(None, "seq", None),
            P(None, "seq", None),
            P(),
            P("seq", "head"),
            P("seq", "head"),
            P("seq", "head"),
            P("seq", "head"),
            P("seq", None),
            P(None, "head"),
            P("head"),
            P(None, "head"),
            P(None, "head"),
            P(None, "head"),
            P("head"),
            P("head", "seq"),
            P(),
            P("seq", "head"),
            P("seq", "head"),
            P("head", "seq"),
        ),
        check_vma=False,
    )
```
